32 devices in a mesh: space: 8 (over z, y), wt: 4 (over x, core).
Axes of the slice: x: 2, y: 2, z: 4, core: 2. Of those that a mesh axis runs over, the one named last changes fastest.
Arguments:
- features: bfloat16 [12288, 256], P(('space', 'wt')), may hold values from -6 to 6
- distances: float32 [12288, 64], P(('space', 'wt')), may hold values from 0.9 to 5.9
- neighbours: int32 [12288, 64], P(('space', 'wt')), may hold values from 0 to 575, as said below
- counts: int32 [12288], P(('space', 'wt')), may hold values from 1 to 64, as said below
- rbf_weight: bfloat16 [600, 256], P('wt'), may hold values from -3 to 3
- query_weight: bfloat16 [256, 256], P('wt'), may hold values from -0.375 to 0.375
- key_weight: bfloat16 [256, 256], P('wt'), may hold values from -0.375 to 0.375
- value_weight: bfloat16 [256, 256], P('wt'), may hold values from -0.375 to 0.375
- out_weight: bfloat16 [256, 256], P('wt'), may hold values from -1.5 to 1.5
- gate_weight: bfloat16 [256, 1024], P('wt'), may hold values from -0.375 to 0.375
- up_weight: bfloat16 [256, 1024], P('wt'), may hold values from -0.375 to 0.375
- down_weight: bfloat16 [1024, 256], P('wt'), may hold values from -0.1875 to 0.1875
- attn_gain: bfloat16 [256], P('wt'), may hold values from 0.5 to 1.5
- ffn_gain: bfloat16 [256], P('wt'), may hold values from 0.5 to 1.5
- readout: bfloat16 [256], P('wt'), may hold values from -0.375 to 0.375
- grad_out: bfloat16 [12288, 256], P(('space', 'wt')), may hold values from -6 to 6
- grad_energy: float32 [12288], P(('space', 'wt')), may hold values from -6 to 6
Outputs:
- activations: float32 [12288, 256], P(('space', 'wt'))
- energy: float32 [12288], P(('space', 'wt'))
- grad_features: float32 [12288, 256], P(('space', 'wt'))
- grad_rbf_weight: float32 [600, 256], P('wt')
- grad_query_weight: float32 [256, 256], P('wt')
- grad_key_weight: float32 [256, 256], P('wt')
- grad_value_weight: float32 [256, 256], P('wt')
- grad_out_weight: float32 [256, 256], P('wt')
- grad_gate_weight: float32 [256, 1024], P('wt')
- grad_up_weight: float32 [256, 1024], P('wt')
- grad_down_weight: float32 [1024, 256], P('wt')
- grad_attn_gain: float32 [256], P('wt')
- grad_ffn_gain: float32 [256], P('wt')
- grad_readout: float32 [256], P('wt')
The draws below stay inside these ranges and needn't reach their ends.
Inputs may be any that keep to these rules, and one draw needn't show every extreme that they name: `neighbours`: rows of the lookup table of 576 rows. The atom at place p of its region names only rows p to p + 192; atoms of the first region never name the table's lower 96 rows and atoms of the last region never its upper 96 rows. `counts`: regions differ widely in their mean count.
All inputs are finite; a program needn't handle non-finite values.
Results may differ from the reference program's by a relative error of at most 0.014.
Values may be sent and summed in bfloat16 or wider, within the bound.
No kernel may reach another device: no remote copies, remote signals or barrier semaphores. Data moves between devices by JAX's collectives and lax.ppermute only.
A program may use at most 256 MiB of HBM per device.

```python
import jax
import jax.numpy as jnp
from jax import lax

D = 256
HEADS = 8
HDIM = 32
FF = 1024
NRBF = 600
K = 64
A_DEV = 384
HALO = 96
ATOMS = 12288


def draw_neighbours(key, part):
    key = jax.random.fold_in(key, 11)
    regions = ATOMS // A_DEV
    offsets = jax.random.randint(key, (ATOMS, K), -HALO, HALO + 1)
    place = jnp.arange(ATOMS, dtype=jnp.int32) % A_DEV
    region = jnp.arange(ATOMS, dtype=jnp.int32) // A_DEV
    position = HALO + place[:, None] + offsets
    position = jnp.where(region[:, None] == 0, jnp.maximum(position, HALO), position)
    position = jnp.where(region[:, None] == regions - 1, jnp.minimum(position, HALO + A_DEV - 1), position)
    slot_ids = jnp.arange(K, dtype=jnp.int32)[None, :]
    lowest = (place[:, None] == 0) & (region[:, None] > 0) & (slot_ids == 0)
    highest = (place[:, None] == A_DEV - 1) & (region[:, None] < regions - 1) & (slot_ids == 0)
    position = jnp.where(lowest, 0, position)
    position = jnp.where(highest, A_DEV + 2 * HALO - 1, position)
    return position.astype(jnp.int32)


def draw_counts(key, part):
    key = jax.random.fold_in(key, 23)
    first_key, second_key, third_key = jax.random.split(key, 3)
    regions = ATOMS // A_DEV
    slab_region = jax.random.randint(first_key, (regions,), 0, 4) == 0
    crowded = jax.random.randint(second_key, (ATOMS,), 3 * K // 4, K + 1)
    sparse_rows = jax.random.randint(third_key, (ATOMS,), K // 4 + 1, K // 2 + 1)
    region = jnp.arange(ATOMS, dtype=jnp.int32) // A_DEV
    result = jnp.where(slab_region[region], crowded, sparse_rows)
    result = result.at[0].set(K).at[1].set(1)
    return result.astype(jnp.int32)


def level_of(rng, dims, cuts, least, top_value):
    factor_of, own = 1.0, jax.random.fold_in(rng, 6)
    for dim, blocks in cuts:
        heights = jnp.exp(jax.random.uniform(jax.random.fold_in(own, dim), (blocks,), jnp.float32, least / len(cuts), top_value / len(cuts)))
        factor_of = factor_of * jnp.repeat(heights, dims[dim] // blocks).reshape([-1 if axis == dim else 1 for axis in range(len(dims))])
    return factor_of


def normal_values(own_key, extent, deviation, most, shards=(), kind=jnp.bfloat16):
    drawn = jax.random.normal(own_key, extent, jnp.float32) * deviation
    if len(shards) > 0:
        drawn = level_of(own_key, extent, shards, -0.22, 0.18) * drawn
    return jnp.clip(drawn, min=-most, max=most).astype(kind)


def setup_inputs(seed: int = 0) -> dict:
    arg_keys = jax.random.split(jax.random.key(seed), 18)
    features = normal_values(arg_keys[0], (ATOMS, D), 1.0, 6.0, ((0, 32),))
    distances = jnp.clip(0.9 + 5 * jax.random.uniform(arg_keys[1], (ATOMS, K), jnp.float32) ** level_of(arg_keys[1], (ATOMS, K), ((0, 32),), -0.2, 0.2), 0.9, 5.9)
    neighbours = draw_neighbours(jax.random.fold_in(arg_keys[17], 71), 0)
    counts = draw_counts(jax.random.fold_in(arg_keys[17], 71), 0)
    rbf_weight = normal_values(arg_keys[4], (NRBF, D), 4 ** -0.5, 3.0, ((0, 4),))
    query_weight = normal_values(arg_keys[5], (D, D), D ** -0.5, 0.375, ((0, 4),))
    key_weight = normal_values(arg_keys[6], (D, D), D ** -0.5, 0.375, ((0, 4),))
    value_weight = normal_values(arg_keys[7], (D, D), D ** -0.5, 0.375, ((0, 4),))
    out_weight = normal_values(arg_keys[8], (D, D), (D // 16) ** -0.5, 1.5, ((0, 4),))
    gate_weight = normal_values(arg_keys[9], (D, FF), D ** -0.5, 0.375, ((0, 4),))
    up_weight = normal_values(arg_keys[10], (D, FF), D ** -0.5, 0.375, ((0, 4),))
    down_weight = normal_values(arg_keys[11], (FF, D), FF ** -0.5, 0.1875, ((0, 4),))
    attn_gain = jnp.clip(1.0 + 0.1 * jax.random.normal(arg_keys[12], (D,), jnp.float32), 0.5, 1.5).astype(jnp.bfloat16)
    ffn_gain = jnp.clip(1.0 + 0.1 * jax.random.normal(arg_keys[13], (D,), jnp.float32), 0.5, 1.5).astype(jnp.bfloat16)
    readout = normal_values(arg_keys[14], (D,), D ** -0.5, 0.375, ((0, 4),))
    grad_out = normal_values(arg_keys[15], (ATOMS, D), 1.0, 6.0, ((0, 32),))
    grad_energy = normal_values(arg_keys[16], (ATOMS,), 1.0, 6.0, ((0, 32),), jnp.float32)
    return {"features": features, "distances": distances, "neighbours": neighbours, "counts": counts, "rbf_weight": rbf_weight, "query_weight": query_weight, "key_weight": key_weight, "value_weight": value_weight, "out_weight": out_weight, "gate_weight": gate_weight, "up_weight": up_weight, "down_weight": down_weight, "attn_gain": attn_gain, "ffn_gain": ffn_gain, "readout": readout, "grad_out": grad_out, "grad_energy": grad_energy}


EPSILON = 1e-06
CUTOFF = 6.0

@jax.custom_vjp
def low(v):
    return lax.optimization_barrier(v.astype(jnp.bfloat16)).astype(jnp.float32)

@jax.custom_vjp
def low_back(v):
    return v

def low_keep(v):
    return (low(v), None)

def low_pass(kept, grad):
    return (grad,)

def back_keep(v):
    return (v, None)

def back_low(kept, grad):
    return (low(grad),)
low.defvjp(low_keep, low_pass)
low_back.defvjp(back_keep, back_low)

def round_both(value):
    return low_back(low(value))

def matmul(left, right):
    return jnp.dot(left, right, precision=lax.Precision.HIGHEST, preferred_element_type=jnp.float32)

def rms_norm(value, gain):
    return value * lax.rsqrt(lax.optimization_barrier(jnp.mean(value * value, -1, keepdims=True)) + EPSILON) * gain

def radial_basis(distances):
    centers = jnp.arange(NRBF, dtype=jnp.float32) * (CUTOFF / NRBF)
    spread = 2.0 * CUTOFF / NRBF
    envelope = 0.5 * (jnp.cos(jnp.pi * distances / CUTOFF) + 1.0)
    return jnp.exp(-0.5 * jnp.square((distances[..., None] - centers) / spread)) * envelope[..., None]

def forward(features, rbf_weight, query_weight, key_weight, value_weight, out_weight, gate_weight, up_weight, down_weight, attn_gain, ffn_gain, readout, distances, neighbours, counts):
    regions = ATOMS // A_DEV
    normed = low(rms_norm(features, attn_gain))
    padding = jnp.zeros((HALO, D), jnp.float32)
    padded = jnp.concatenate([padding, normed, padding], 0)
    score_scale = HDIM ** (-0.5)

    def region_step(packed):
        region_index, own_rows, distance_block, neighbour_block, count_block = packed
        lookup = lax.dynamic_slice_in_dim(padded, region_index * A_DEV, A_DEV + 2 * HALO, 0)
        basis_rows = low(radial_basis(distance_block)).reshape(A_DEV * K, NRBF)
        gathered = lookup[neighbour_block.reshape(-1)]
        edge_input = round_both(gathered + matmul(basis_rows, rbf_weight))
        queries = round_both(matmul(lookup[HALO:HALO + A_DEV], query_weight)).reshape(A_DEV, HEADS, HDIM)
        key_heads = round_both(matmul(edge_input, key_weight)).reshape(A_DEV, K, HEADS, HDIM)
        value_heads = round_both(matmul(edge_input, value_weight)).reshape(A_DEV, K, HEADS, HDIM)
        scores = jnp.einsum('ahd,akhd->ahk', queries, key_heads, precision=lax.Precision.HIGHEST) * score_scale
        usable = jnp.arange(K, dtype=jnp.int32)[None, None, :] < count_block[:, None, None]
        scores = jnp.where(usable, scores, -1e+30)
        soft_weights = jax.nn.softmax(scores, -1)
        attended = jnp.einsum('ahk,akhd->ahd', low(soft_weights), value_heads, precision=lax.Precision.HIGHEST)
        attended = round_both(attended).reshape(A_DEV, D)
        residual = own_rows + low_back(matmul(attended, out_weight))
        hidden_in = round_both(rms_norm(residual, ffn_gain))
        gate_pre = low_back(matmul(hidden_in, gate_weight))
        up_pre = low_back(matmul(hidden_in, up_weight))
        activated = low(jax.nn.silu(gate_pre) * up_pre)
        outputs = residual + low_back(matmul(activated, down_weight))
        return (outputs, lax.optimization_barrier(jnp.sum(outputs * readout, -1)))
    packed_all = (jnp.arange(regions, dtype=jnp.int32), features.reshape(regions, A_DEV, D), distances.reshape(regions, A_DEV, K), neighbours.reshape(regions, A_DEV, K), counts.reshape(regions, A_DEV))
    outputs, energy = lax.map(jax.checkpoint(region_step), packed_all)
    return (outputs.reshape(ATOMS, D), energy.reshape(ATOMS))

def reference(features, distances, neighbours, counts, rbf_weight, query_weight, key_weight, value_weight, out_weight, gate_weight, up_weight, down_weight, attn_gain, ffn_gain, readout, grad_out, grad_energy):
    floats = tuple((entry.astype(jnp.float32) for entry in (features, rbf_weight, query_weight, key_weight, value_weight, out_weight, gate_weight, up_weight, down_weight, attn_gain, ffn_gain, readout)))

    def wrapped(*inputs):
        return forward(*inputs, distances, neighbours, counts)
    (outputs, energy), pullback = jax.vjp(wrapped, *floats)
    gradients = pullback((grad_out.astype(jnp.float32), grad_energy.astype(jnp.float32)))
    return (outputs, energy, gradients[0], gradients[1], gradients[2], gradients[3], gradients[4], gradients[5], gradients[6], gradients[7], gradients[8], gradients[9], gradients[10], gradients[11])
```

```python
import functools
import math

import jax
import jax.numpy as jnp
from jax import lax
from jax.experimental import pallas as pl
from jax.experimental.pallas import tpu as pltpu
from jax.sharding import PartitionSpec as P

HEADS = 8
HALO = 96
EPSILON = 1e-06
CUTOFF = 6.0

BLOCK = 64
PAIRS = BLOCK // 2
LANES = 128
TILE = 256
GROUP = 1024

BF16 = jnp.bfloat16
F32 = jnp.float32


def nn(a, b):
    return lax.dot_general(a, b, (((1,), (0,)), ((), ())), preferred_element_type=F32)


def nt(a, b):
    return lax.dot_general(a, b, (((1,), (1,)), ((), ())), preferred_element_type=F32)


def tn(a, b):
    return lax.dot_general(a, b, (((0,), (0,)), ((), ())), preferred_element_type=F32)


def round_up(value, step):
    return -(-value // step) * step


def rms(value):
    inverse = lax.rsqrt(jnp.mean(value * value, -1, keepdims=True) + EPSILON)
    return value * inverse, inverse


def norm_back(grad_normed, normed_rows, inverse):
    return inverse * (
        grad_normed - normed_rows * jnp.mean(grad_normed * normed_rows, -1, keepdims=True)
    )


def pair_rows(block):
    return jnp.concatenate([block[:PAIRS], block[PAIRS:]], axis=1)


def head_of_lane(width):
    return lax.broadcasted_iota(jnp.int32, (1, width), 1) // (width // HEADS)


def spread_heads(rows, out_ref):
    atoms, width = rows.shape
    heads = head_of_lane(width)
    for start in range(0, atoms, PAIRS):
        block, side = start // BLOCK, (start % BLOCK) // PAIRS
        part = rows[start : start + PAIRS]
        for head in range(HEADS):
            place = block * BLOCK * HEADS + side * HEADS + head
            kept = jnp.where(heads == head, part, 0.0)
            for half in range(width // LANES):
                out_ref[half, pl.ds(place, PAIRS, stride=2 * HEADS), :] = kept[
                    :, half * LANES : (half + 1) * LANES
                ]


def wide(ref, rows=slice(None)):
    return jnp.concatenate([ref[half, rows, :] for half in range(ref.shape[0])], axis=1)


def gather_heads(rows_ref, weight, atoms):
    width = weight.shape[1]
    heads = head_of_lane(width)
    total = None
    for head in range(HEADS):
        parts = []
        for start in range(0, atoms, PAIRS):
            block, side = start // BLOCK, (start % BLOCK) // PAIRS
            place = block * BLOCK * HEADS + side * HEADS + head
            parts.append(wide(rows_ref, pl.ds(place, PAIRS, stride=2 * HEADS)))
        left = jnp.concatenate(parts, axis=0).astype(BF16)
        right = jnp.where(heads == head, weight, jnp.zeros_like(weight))
        term = nn(left, right)
        total = term if total is None else total + term
    return total


def half_sums(value, low_half, op, neutral):
    low = op(jnp.where(low_half, value, neutral), axis=1, keepdims=True)
    high = op(jnp.where(low_half, neutral, value), axis=1, keepdims=True)
    return jnp.where(low_half, low, high)


def write_onehot(neighbours_ref, first_row, onehot_ref):
    rows = onehot_ref.shape[0]
    relative = pair_rows(neighbours_ref[...]) - first_row
    relative = relative.astype(F32)
    places = lax.broadcasted_iota(jnp.int32, (rows, LANES), 0).astype(F32)
    for pair in range(PAIRS):
        hit = places == relative[pair : pair + 1, :]
        onehot_ref[:, pair * LANES : (pair + 1) * LANES] = jnp.where(hit, 1.0, 0.0).astype(BF16)


def diagonal(tile, low_half):
    first = jnp.where(low_half, tile[0:8, :LANES], tile[8:16, :LANES])
    second = jnp.where(low_half, tile[16:24, LANES:], tile[24:32, LANES:])
    return first, second


def block_rows(value, low_half):
    zero = jnp.zeros_like(value)
    return jnp.concatenate(
        [jnp.where(low_half, value, zero), jnp.where(low_half, zero, value)], axis=0
    ).astype(BF16)


def basis_kernel(shard, padded, spread, step, dist_ref, out_ref, scaled_ref, env_ref):
    dist = pair_rows(dist_ref[...])
    factor = math.sqrt(0.5 / math.log(2.0)) / spread
    scaled_ref[...] = dist * factor
    env_ref[...] = 0.5 * (jnp.cos(jnp.pi * dist / CUTOFF) + 1.0)
    rows = out_ref.shape[0]
    iota = lax.broadcasted_iota(jnp.int32, (16, LANES), 0).astype(F32) * (step * factor)

    @pl.loop(0, PAIRS)
    def _(pair):
        base = scaled_ref[pl.ds(pair, 1), :] - iota
        envelope = jnp.broadcast_to(env_ref[pl.ds(pair, 1), :], (16, LANES))
        lanes = pl.ds(pl.multiple_of(pair * LANES, LANES), LANES)
        for row in range(0, rows, 16):
            center = (row // padded) * shard + row % padded
            delta = base - (center * step * factor)
            value = jnp.exp2(-(delta * delta)) * envelope
            out_ref[row : row + 16, lanes] = value.astype(BF16)


def basis_call(distances, shard, padded, members, basis_count):
    atoms, slots = distances.shape
    blocks = atoms // BLOCK
    rows = members * padded
    edges = BLOCK * slots
    return pl.pallas_call(
        functools.partial(
            basis_kernel, shard, padded, 2.0 * CUTOFF / basis_count, CUTOFF / basis_count
        ),
        grid=(blocks,),
        out_shape=jax.ShapeDtypeStruct((blocks, rows, edges), BF16),
        in_specs=[pl.BlockSpec((BLOCK, slots), lambda b: (b, 0))],
        out_specs=pl.BlockSpec((None, rows, edges), lambda b: (b, 0, 0)),
        scratch_shapes=[pltpu.VMEM((PAIRS, LANES), F32), pltpu.VMEM((PAIRS, LANES), F32)],
        compiler_params=pltpu.CompilerParams(vmem_limit_bytes=40 * 2**20),
        cost_estimate=pl.CostEstimate(
            flops=8 * atoms * slots * rows,
            bytes_accessed=2 * atoms * slots * rows,
            transcendentals=atoms * slots * rows,
        ),
        name="radial_basis",
    )(distances)


def place_shards(index_ref, packs, row, count, stride, out_ref):
    me = index_ref[0]
    for offset, pack in enumerate(packs):
        owner = lax.bitwise_xor(me, offset)
        start = pl.multiple_of(owner * stride, 16)
        out_ref[pl.ds(start, count), :] = pack[row : row + count, :]


def vector_of(packs, row):
    total = packs[0][row : row + 1, :].astype(F32)
    for pack in packs[1:]:
        total = total + pack[row : row + 1, :].astype(F32)
    return total


def forward_kernel(
    padded,
    quarter,
    scale,
    index_ref,
    counts_ref,
    features_ref,
    before_ref,
    after_ref,
    pack0,
    pack1,
    pack2,
    pack3,
    neighbours_ref,
    basis_ref,
    edge_ref,
    soft_ref,
    attended_ref,
    pooled_ref,
    lookup_ref,
    query_ref,
    kvq_ref,
    weight_t,
    assembled,
    spread,
    keyed,
    onehot,
    bands,
    pooled,
):
    step = pl.program_id(0)
    packs = (pack0, pack1, pack2, pack3)
    atoms, width = features_ref.shape
    low_half = lax.broadcasted_iota(jnp.int32, (1, LANES), 1) < LANES // 2
    lane = lax.broadcasted_iota(jnp.int32, (1, LANES), 1)
    edges = basis_ref.shape[1]

    @pl.when(step == 0)
    def _():
        place_shards(index_ref, packs, 0, padded, padded, assembled)
        weight_t[...] = assembled[...].astype(F32).T.astype(BF16)
        for which in range(3):
            place_shards(
                index_ref, packs, padded + which * quarter, quarter, quarter, kvq_ref.at[which]
            )
        gain = vector_of(packs, padded + 3 * quarter)
        for ref, start in ((before_ref, 0), (features_ref, HALO), (after_ref, HALO + atoms)):
            normed, _ = rms(ref[...].astype(F32))
            lookup_ref[start : start + ref.shape[0], :] = (normed * gain).astype(BF16)
        query = nn(lookup_ref[HALO : HALO + atoms, :], kvq_ref[0]).astype(BF16)
        query_ref[...] = query
        spread_heads(query.astype(F32), spread)
        keyed[...] = (nt(wide(spread).astype(BF16), kvq_ref[1]) * scale).astype(BF16)
        bands[...] = jnp.zeros_like(bands)

    first_row = step * BLOCK
    write_onehot(neighbours_ref, first_row, onehot)
    window = lookup_ref[pl.ds(pl.multiple_of(first_row, BLOCK), onehot.shape[0]), :]
    window_t = window.astype(F32).T.astype(BF16)
    for group in range(edges // GROUP):
        part = slice(group * GROUP, (group + 1) * GROUP)
        edge_ref[:, part] = (
            nn(weight_t[...], basis_ref[:, part]) + nn(window_t, onehot[:, part])
        ).astype(BF16)
    rows = BLOCK * HEADS
    base = pl.multiple_of(step * rows, rows)
    for tile in range(edges // TILE):
        part = slice(tile * TILE, (tile + 1) * TILE)
        left = keyed[pl.ds(base + tile * 32, 32), :]
        both = diagonal(nn(left, edge_ref[:, part]), low_half)
        for side, score in enumerate(both):
            pair = 2 * tile + side
            low_count = counts_ref[step * BLOCK + pair]
            high_count = counts_ref[step * BLOCK + PAIRS + pair]
            usable = lane < jnp.where(low_half, low_count, high_count + LANES // 2)
            score = jnp.where(usable, score, -1e30)
            top = half_sums(score, low_half, jnp.max, -jnp.inf)
            power = jnp.exp(score - top)
            soft = power / half_sums(power, low_half, jnp.sum, 0.0)
            soft_ref[:, pair * LANES : (pair + 1) * LANES] = soft
            bands[tile, side * 16 : side * 16 + 16, side * LANES : (side + 1) * LANES] = (
                block_rows(soft, low_half)
            )
        result = nt(bands[tile], edge_ref[:, part])
        for half in range(width // LANES):
            pooled[half, pl.ds(base + tile * 32, 32), :] = result[
                :, half * LANES : (half + 1) * LANES
            ]

    @pl.when(step == pl.num_programs(0) - 1)
    def _():
        attended_ref[...] = gather_heads(pooled, kvq_ref[2], atoms).astype(BF16)
        pooled_ref[...] = wide(pooled).astype(BF16)


def forward_call(index, counts, features, before, after, packs, neighbours, basis, padded, quarter):
    atoms, width = features.shape
    slots = neighbours.shape[1]
    blocks, rows, edges = basis.shape
    table = atoms + 2 * HALO
    full = lambda shape: pl.BlockSpec(shape, lambda b: (0,) * len(shape))
    head_rows = atoms * HEADS
    window = BLOCK + 2 * HALO
    return pl.pallas_call(
        functools.partial(forward_kernel, padded, quarter, (width // HEADS) ** -0.5),
        grid=(blocks,),
        out_shape=(
            jax.ShapeDtypeStruct((blocks, width, edges), BF16),
            jax.ShapeDtypeStruct((blocks, HEADS, edges), F32),
            jax.ShapeDtypeStruct((atoms, width), BF16),
            jax.ShapeDtypeStruct((head_rows, width), BF16),
            jax.ShapeDtypeStruct((table, width), BF16),
            jax.ShapeDtypeStruct((atoms, width), BF16),
            jax.ShapeDtypeStruct((3, width, width), BF16),
        ),
        in_specs=[
            pl.BlockSpec(memory_space=pltpu.SMEM),
            pl.BlockSpec(memory_space=pltpu.SMEM),
            full((atoms, width)),
            full((HALO, width)),
            full((HALO, width)),
        ]
        + [full(pack.shape) for pack in packs]
        + [
            pl.BlockSpec((BLOCK, slots), lambda b: (b, 0)),
            pl.BlockSpec((None, rows, edges), lambda b: (b, 0, 0)),
        ],
        out_specs=(
            pl.BlockSpec((None, width, edges), lambda b: (b, 0, 0)),
            pl.BlockSpec((None, HEADS, edges), lambda b: (b, 0, 0)),
            full((atoms, width)),
            full((head_rows, width)),
            full((table, width)),
            full((atoms, width)),
            full((3, width, width)),
        ),
        scratch_shapes=[
            pltpu.VMEM((width, rows), BF16),
            pltpu.VMEM((rows, width), BF16),
            pltpu.VMEM((width // LANES, head_rows, LANES), F32),
            pltpu.VMEM((head_rows, width), BF16),
            pltpu.VMEM((window, edges), BF16),
            pltpu.VMEM((edges // TILE, 32, TILE), BF16),
            pltpu.VMEM((width // LANES, head_rows, LANES), F32),
        ],
        compiler_params=pltpu.CompilerParams(vmem_limit_bytes=58 * 2**20),
        cost_estimate=pl.CostEstimate(
            flops=2 * atoms * slots * width * (rows + window + 64),
            bytes_accessed=2 * atoms * slots * (rows + width),
            transcendentals=atoms * slots * HEADS,
        ),
        name="attention_forward",
    )(index, counts, features, before, after, *packs, neighbours, basis)


def ffn_kernel(
    quarter,
    small_row,
    index_ref,
    features_ref,
    attended_ref,
    grad_out_ref,
    grad_energy_ref,
    small0,
    small1,
    small2,
    small3,
    pack0,
    pack1,
    pack2,
    pack3,
    out_ref,
    energy_ref,
    grad_residual_ref,
    grad_attended_ref,
    grads_ref,
    sums_ref,
    w_gate,
    w_up,
    w_down,
    w_out,
):
    small = (small0, small1, small2, small3)
    packs = (pack0, pack1, pack2, pack3)
    atoms, width = features_ref.shape
    parts = w_gate.shape[1] // width
    down_rows = w_down.shape[0] // 4
    me = index_ref[0]
    for offset, pack in enumerate(packs):
        owner = lax.bitwise_xor(me, offset)
        rows = pl.ds(pl.multiple_of(owner * quarter, 16), quarter)
        for part in range(parts):
            lanes = slice(part * width, (part + 1) * width)
            w_gate[rows, lanes] = pack[part * quarter : (part + 1) * quarter, :]
            w_up[rows, lanes] = pack[(parts + part) * quarter : (parts + part + 1) * quarter, :]
        start = 2 * parts * quarter
        w_down[pl.ds(pl.multiple_of(owner * down_rows, 16), down_rows), :] = pack[
            start : start + down_rows, :
        ]
        w_out[rows, :] = pack[start + down_rows : start + down_rows + quarter, :]
    gain = vector_of(small, small_row + 1)
    readout = vector_of(small, small_row + 2)

    attended = attended_ref[...]
    residual = features_ref[...].astype(F32) + nn(attended, w_out[...])
    normed, inverse = rms(residual)
    hidden = (normed * gain).astype(BF16)
    gate = nn(hidden, w_gate[...])
    up = nn(hidden, w_up[...])
    sigmoid = jax.nn.sigmoid(gate)
    silu = gate * sigmoid
    activated = (silu * up).astype(BF16)
    outputs = residual + nn(activated, w_down[...])
    out_ref[...] = outputs
    energy_ref[...] = jnp.sum(outputs * readout, -1, keepdims=True)
    grad_energy = grad_energy_ref[...]
    grad_act = grad_out_ref[...].astype(F32) + grad_energy * readout
    grad_branch = grad_act.astype(BF16)
    grad_down = tn(activated, grad_branch)
    grad_activated = nt(grad_branch, w_down[...])
    grad_gate = (grad_activated * up * sigmoid * (1.0 + gate * (1.0 - sigmoid))).astype(BF16)
    grad_up = (grad_activated * silu).astype(BF16)
    grad_gate_w = tn(hidden, grad_gate)
    grad_up_w = tn(hidden, grad_up)
    grad_hidden = (nt(grad_gate, w_gate[...]) + nt(grad_up, w_up[...])).astype(BF16).astype(F32)
    grad_residual = grad_act + norm_back(grad_hidden * gain, normed, inverse)
    grad_residual_ref[...] = grad_residual
    grad_proj = grad_residual.astype(BF16)
    grad_attended_ref[...] = nt(grad_proj, w_out[...]).astype(BF16)
    grad_out_w = tn(attended, grad_proj)
    for owner in range(4):
        rows = slice(owner * quarter, (owner + 1) * quarter)
        for part in range(parts):
            lanes = slice(part * width, (part + 1) * width)
            grads_ref[owner, part * quarter : (part + 1) * quarter, :] = grad_gate_w[
                rows, lanes
            ].astype(BF16)
            grads_ref[owner, (parts + part) * quarter : (parts + part + 1) * quarter, :] = (
                grad_up_w[rows, lanes].astype(BF16)
            )
        start = 2 * parts * quarter
        grads_ref[owner, start : start + down_rows, :] = grad_down[
            owner * down_rows : (owner + 1) * down_rows, :
        ].astype(BF16)
        grads_ref[owner, start + down_rows : start + down_rows + quarter, :] = grad_out_w[
            rows, :
        ].astype(BF16)
    sums_ref[...] = jnp.zeros_like(sums_ref)
    sums_ref[1:2, :] = jnp.sum(grad_hidden * normed, 0, keepdims=True)
    sums_ref[2:3, :] = jnp.sum(grad_energy * outputs, 0, keepdims=True)


def ffn_call(index, features, attended, grad_out, grad_energy, small, packs, hidden, quarter, row):
    atoms, width = features.shape
    vmem = pl.BlockSpec(memory_space=pltpu.VMEM)
    return pl.pallas_call(
        functools.partial(ffn_kernel, quarter, row),
        out_shape=(
            jax.ShapeDtypeStruct((atoms, width), F32),
            jax.ShapeDtypeStruct((atoms, 1), F32),
            jax.ShapeDtypeStruct((atoms, width), F32),
            jax.ShapeDtypeStruct((atoms, width), BF16),
            jax.ShapeDtypeStruct((4,) + packs[0].shape, BF16),
            jax.ShapeDtypeStruct((8, width), F32),
        ),
        in_specs=[pl.BlockSpec(memory_space=pltpu.SMEM)] + [vmem] * 12,
        out_specs=(vmem,) * 6,
        scratch_shapes=[
            pltpu.VMEM((width, hidden), BF16),
            pltpu.VMEM((width, hidden), BF16),
            pltpu.VMEM((hidden, width), BF16),
            pltpu.VMEM((width, width), BF16),
        ],
        compiler_params=pltpu.CompilerParams(vmem_limit_bytes=58 * 2**20),
        cost_estimate=pl.CostEstimate(
            flops=18 * atoms * width * hidden, bytes_accessed=2**23, transcendentals=atoms * hidden
        ),
        name="feed_forward",
    )(index, features, attended, grad_out, grad_energy, *small, *packs)


def backward_kernel(
    padded,
    quarter,
    scale,
    gain_row,
    features_ref,
    before_ref,
    after_ref,
    small0,
    small1,
    small2,
    small3,
    lookup_ref,
    query_ref,
    kvq_ref,
    pooled_ref,
    grad_attended_ref,
    grad_residual_ref,
    sums_ref,
    neighbours_ref,
    basis_ref,
    edge_ref,
    soft_ref,
    grads_ref,
    grad_own_ref,
    grad_halo_ref,
    spread_q,
    spread_g,
    valued,
    mixed_t,
    onehot,
    bands,
    grad_edge,
    pooled,
    grad_rbf,
    grad_lookup,
):
    step = pl.program_id(0)
    small = (small0, small1, small2, small3)
    atoms, width = features_ref.shape
    low_half = lax.broadcasted_iota(jnp.int32, (1, LANES), 1) < LANES // 2
    edges = basis_ref.shape[1]
    group_rows = GROUP // 64 * HEADS
    groups = edges // GROUP

    @pl.when(step == 0)
    def _():
        spread_heads(query_ref[...].astype(F32), pooled)
        spread_q[...] = wide(pooled).astype(BF16)
        spread_heads(grad_attended_ref[...].astype(F32), pooled)
        spread_g[...] = wide(pooled).astype(BF16)
        valued[...] = nt(spread_g[...], kvq_ref[2]).astype(BF16)
        for group in range(mixed_t.shape[0]):
            rows = slice(group * group_rows, (group + 1) * group_rows)
            mixed_t[group, :, :group_rows] = (nt(kvq_ref[1], spread_q[rows, :]) * scale).astype(
                BF16
            )
            mixed_t[group, :, group_rows:] = nt(kvq_ref[2], spread_g[rows, :]).astype(BF16)
        bands[...] = jnp.zeros_like(bands)
        grad_rbf[...] = jnp.zeros_like(grad_rbf)
        grad_lookup[...] = jnp.zeros_like(grad_lookup)

    first_row = step * BLOCK
    write_onehot(neighbours_ref, first_row, onehot)
    rows = BLOCK * HEADS
    base = pl.multiple_of(step * rows, rows)
    for tile in range(edges // TILE):
        part = slice(tile * TILE, (tile + 1) * TILE)
        group, place = tile * TILE // GROUP, tile * TILE % GROUP
        left = valued[pl.ds(base + tile * 32, 32), :]
        both = diagonal(nn(left, edge_ref[:, part]), low_half)
        for side, grad_soft in enumerate(both):
            pair = 2 * tile + side
            soft = soft_ref[:, pair * LANES : (pair + 1) * LANES]
            mean = half_sums(soft * grad_soft, low_half, jnp.sum, 0.0)
            grad_score = soft * (grad_soft - mean)
            lanes = slice(place + side * LANES, place + (side + 1) * LANES)
            row = place // TILE * 32 + side * 16
            bands[group, row : row + 16, lanes] = block_rows(grad_score, low_half)
            bands[group, group_rows + row : group_rows + row + 16, lanes] = block_rows(
                soft, low_half
            )
        row = place // TILE * 32
        result = nt(bands[group, row : row + 32, place : place + TILE], edge_ref[:, part])
        for half in range(width // LANES):
            pooled[half, pl.ds(base + tile * 32, 32), :] = result[
                :, half * LANES : (half + 1) * LANES
            ]
    for group in range(groups):
        part = slice(group * GROUP, (group + 1) * GROUP)
        grad_edge[:, part] = nn(mixed_t[step * groups + group], bands[group]).astype(BF16)
    grad_rbf[...] += nt(basis_ref[...], grad_edge[...])
    place = pl.ds(pl.multiple_of(first_row, BLOCK), onehot.shape[0])
    grad_lookup[place, :] += nt(onehot[...], grad_edge[...])

    @pl.when(step == pl.num_programs(0) - 1)
    def _():
        own = slice(HALO, HALO + atoms)
        grad_query = (gather_heads(pooled, kvq_ref[1], atoms) * scale).astype(BF16)
        grad_key_w = tn(wide(pooled).astype(BF16), spread_q[...]) * scale
        grad_value_w = tn(pooled_ref[...], spread_g[...])
        grad_query_w = tn(lookup_ref[own, :], grad_query)
        grad_lookup[own, :] += nt(grad_query, kvq_ref[0])
        gain = vector_of(small, gain_row)
        grad_gain = jnp.zeros((1, width), F32)
        places = (
            (before_ref, 0, grad_halo_ref.at[0]),
            (features_ref, HALO, grad_own_ref),
            (after_ref, HALO + atoms, grad_halo_ref.at[1]),
        )
        for ref, start, out in places:
            normed, inverse = rms(ref[...].astype(F32))
            grad = grad_lookup[start : start + ref.shape[0], :]
            grad_gain = grad_gain + jnp.sum(grad * normed, 0, keepdims=True)
            back = norm_back(grad * gain, normed, inverse)
            if start == HALO:
                back = back + grad_residual_ref[...]
            out[...] = back.astype(out.dtype)
        vectors = jnp.concatenate([grad_gain, sums_ref[1:8, :], jnp.zeros((8, width), F32)], 0)
        for owner in range(4):
            rows = slice(owner * quarter, (owner + 1) * quarter)
            grads_ref[owner, :padded, :] = grad_rbf[
                owner * padded : (owner + 1) * padded, :
            ].astype(BF16)
            for which, grad in enumerate((grad_query_w, grad_key_w, grad_value_w)):
                start = padded + which * quarter
                grads_ref[owner, start : start + quarter, :] = grad[rows, :].astype(BF16)
            start = padded + 3 * quarter
            grads_ref[owner, start : start + 16, :] = vectors.astype(BF16)


def backward_call(
    features,
    before,
    after,
    small,
    lookup,
    query,
    kvq,
    pooled,
    grad_attended,
    grad_residual,
    sums,
    neighbours,
    basis,
    edge,
    soft,
    padded,
    quarter,
):
    atoms, width = features.shape
    slots = neighbours.shape[1]
    blocks, rows, edges = basis.shape
    table = atoms + 2 * HALO
    head_rows = atoms * HEADS
    window = BLOCK + 2 * HALO
    group_rows = GROUP // slots * HEADS
    full = lambda shape: pl.BlockSpec(shape, lambda b: (0,) * len(shape))
    whole = (
        (features, before, after)
        + tuple(small)
        + (lookup, query, kvq, pooled, grad_attended, grad_residual, sums)
    )
    return pl.pallas_call(
        functools.partial(
            backward_kernel, padded, quarter, (width // HEADS) ** -0.5, padded + 3 * quarter
        ),
        grid=(blocks,),
        out_shape=(
            jax.ShapeDtypeStruct((4,) + small[0].shape, BF16),
            jax.ShapeDtypeStruct((atoms, width), F32),
            jax.ShapeDtypeStruct((2, HALO, width), BF16),
        ),
        in_specs=[full(value.shape) for value in whole]
        + [
            pl.BlockSpec((BLOCK, slots), lambda b: (b, 0)),
            pl.BlockSpec((None, rows, edges), lambda b: (b, 0, 0)),
            pl.BlockSpec((None, width, edges), lambda b: (b, 0, 0)),
            pl.BlockSpec((None, HEADS, edges), lambda b: (b, 0, 0)),
        ],
        out_specs=(
            full((4,) + small[0].shape),
            full((atoms, width)),
            full((2, HALO, width)),
        ),
        scratch_shapes=[
            pltpu.VMEM((head_rows, width), BF16),
            pltpu.VMEM((head_rows, width), BF16),
            pltpu.VMEM((head_rows, width), BF16),
            pltpu.VMEM((head_rows // group_rows, width, 2 * group_rows), BF16),
            pltpu.VMEM((window, edges), BF16),
            pltpu.VMEM((edges // GROUP, 2 * group_rows, GROUP), BF16),
            pltpu.VMEM((width, edges), BF16),
            pltpu.VMEM((width // LANES, head_rows, LANES), F32),
            pltpu.VMEM((rows, width), F32),
            pltpu.VMEM((table, width), F32),
        ],
        compiler_params=pltpu.CompilerParams(vmem_limit_bytes=60 * 2**20),
        cost_estimate=pl.CostEstimate(
            flops=2 * atoms * slots * width * (rows + window + 384),
            bytes_accessed=2 * atoms * slots * (rows + width),
            transcendentals=0,
        ),
        name="attention_backward",
    )(*whole, neighbours, basis, edge, soft)


def exchange(value, axis, offset):
    size = lax.axis_size(axis)
    return lax.ppermute(value, axis, [(i, i ^ offset) for i in range(size)])


def shifted(value, by):
    axes = ("space", "wt")
    size = lax.axis_size(axes)
    pairs = [(i, i + by) for i in range(size) if 0 <= i + by < size]
    return lax.ppermute(value, axes, pairs)


def gathered(value):
    return [value] + [exchange(value, "wt", offset) for offset in range(1, lax.axis_size("wt"))]


def reduced(partials):
    me = lax.axis_index("wt")
    take = lambda owner: lax.dynamic_index_in_dim(partials, owner, 0, keepdims=False)
    total = take(me).astype(F32)
    for offset in range(1, lax.axis_size("wt")):
        total = total + exchange(take(me ^ offset), "wt", offset).astype(F32)
    offset = 1
    while offset < lax.axis_size("space"):
        sent = total.astype(BF16)
        total = sent.astype(F32) + exchange(sent, "space", offset).astype(F32)
        offset *= 2
    return total


def local(
    features,
    distances,
    neighbours,
    counts,
    rbf_weight,
    query_weight,
    key_weight,
    value_weight,
    out_weight,
    gate_weight,
    up_weight,
    down_weight,
    attn_gain,
    ffn_gain,
    readout,
    grad_out,
    grad_energy,
):
    members = lax.axis_size("wt")
    atoms, width = features.shape
    shard = rbf_weight.shape[0]
    padded = round_up(shard, 16)
    quarter = query_weight.shape[0]
    hidden = gate_weight.shape[1]
    parts = hidden // width
    me = lax.axis_index("wt").astype(jnp.int32)
    index = me[None]

    vectors = jnp.zeros((16, width), BF16)
    vectors = lax.dynamic_update_slice(
        vectors, jnp.stack([attn_gain, ffn_gain, readout]), (0, me * quarter)
    )
    small = jnp.concatenate(
        [
            jnp.pad(rbf_weight, ((0, padded - shard), (0, 0))),
            query_weight,
            key_weight,
            value_weight,
            vectors,
        ],
        0,
    )
    columns = lambda value: [value[:, part * width : (part + 1) * width] for part in range(parts)]
    large = jnp.concatenate(
        columns(gate_weight) + columns(up_weight) + [down_weight, out_weight], 0
    )
    before = shifted(features[atoms - HALO :], 1)
    after = shifted(features[:HALO], -1)
    small_all = gathered(small)
    basis = basis_call(distances, shard, padded, members, members * shard)
    large_all = gathered(large)

    edge, soft, attended, pooled, lookup, query, kvq = forward_call(
        index, counts, features, before, after, small_all, neighbours, basis, padded, quarter
    )
    gain_row = padded + 3 * quarter
    outputs, energy, grad_residual, grad_attended, large_grads, sums = ffn_call(
        index,
        features,
        attended,
        grad_out,
        grad_energy[:, None],
        small_all,
        large_all,
        hidden,
        quarter,
        gain_row,
    )
    small_grads, grad_own, grad_halo = backward_call(
        features,
        before,
        after,
        small_all,
        lookup,
        query,
        kvq,
        pooled,
        grad_attended,
        grad_residual,
        sums,
        neighbours,
        basis,
        edge,
        soft,
        padded,
        quarter,
    )
    from_upper = shifted(grad_halo[0], -1).astype(F32)
    from_lower = shifted(grad_halo[1], 1).astype(F32)
    grad_features = grad_own.at[:HALO].add(from_lower)
    grad_features = grad_features.at[atoms - HALO :].add(from_upper)
    large_sum = reduced(large_grads)
    small_sum = reduced(small_grads)
    start = 2 * parts * quarter
    down_rows = down_weight.shape[0]
    columns_of = lambda first: jnp.concatenate(
        [large_sum[first + part * quarter : first + (part + 1) * quarter] for part in range(parts)],
        1,
    )
    piece = lambda which: small_sum[padded + which * quarter : padded + (which + 1) * quarter]
    vector = lambda row: lax.dynamic_slice(small_sum[gain_row + row], (me * quarter,), (quarter,))
    return (
        outputs,
        energy[:, 0],
        grad_features,
        small_sum[:shard],
        piece(0),
        piece(1),
        piece(2),
        large_sum[start + down_rows : start + down_rows + quarter],
        columns_of(0),
        columns_of(parts * quarter),
        large_sum[start : start + down_rows],
        vector(0),
        vector(1),
        vector(2),
    )


def solution(mesh):
    rows = P(("space", "wt"), None)
    line = P(("space", "wt"))
    in_specs = (rows, rows, rows, line) + (P("wt", None),) * 8 + (P("wt"),) * 3 + (rows, line)
    out_specs = (rows, line, rows) + (P("wt", None),) * 8 + (P("wt"),) * 3
    return jax.shard_map(local, mesh=mesh, in_specs=in_specs, out_specs=out_specs, check_vma=False)
```

```python
import functools
import math

import jax
import jax.numpy as jnp
from jax import lax
from jax.experimental import pallas as pl
from jax.experimental.pallas import tpu as pltpu
from jax.sharding import PartitionSpec as P

HEADS = 8
HALO = 96
EPSILON = 1e-06
CUTOFF = 6.0

BLOCK = 64
PAIRS = BLOCK // 2
LANES = 128
TILE = 256
GROUP = 1024

BF16 = jnp.bfloat16
F32 = jnp.float32


def nn(a, b):
    return lax.dot_general(a, b, (((1,), (0,)), ((), ())), preferred_element_type=F32)


def nt(a, b):
    return lax.dot_general(a, b, (((1,), (1,)), ((), ())), preferred_element_type=F32)


def tn(a, b):
    return lax.dot_general(a, b, (((0,), (0,)), ((), ())), preferred_element_type=F32)


def round_up(value, step):
    return -(-value // step) * step


def rms(value):
    inverse = lax.rsqrt(jnp.mean(value * value, -1, keepdims=True) + EPSILON)
    return value * inverse, inverse


def norm_back(grad_normed, normed_rows, inverse):
    return inverse * (
        grad_normed - normed_rows * jnp.mean(grad_normed * normed_rows, -1, keepdims=True)
    )


def pair_rows(block):
    return jnp.concatenate([block[:PAIRS], block[PAIRS:]], axis=1)


def head_of_lane(width):
    return lax.broadcasted_iota(jnp.int32, (1, width), 1) // (width // HEADS)


def spread_heads(rows, out_ref):
    atoms, width = rows.shape
    heads = head_of_lane(width)
    for start in range(0, atoms, PAIRS):
        block, side = start // BLOCK, (start % BLOCK) // PAIRS
        part = rows[start : start + PAIRS]
        for head in range(HEADS):
            place = block * BLOCK * HEADS + side * HEADS + head
            kept = jnp.where(heads == head, part, 0.0)
            for half in range(width // LANES):
                out_ref[half, pl.ds(place, PAIRS, stride=2 * HEADS), :] = kept[
                    :, half * LANES : (half + 1) * LANES
                ]


def wide(ref, rows=slice(None)):
    return jnp.concatenate([ref[half, rows, :] for half in range(ref.shape[0])], axis=1)


def gather_heads(rows_ref, weight, atoms):
    heads = head_of_lane(weight.shape[1])
    lefts, rights = [], []
    for head in range(HEADS):
        parts = []
        for start in range(0, atoms, PAIRS):
            block, side = start // BLOCK, (start % BLOCK) // PAIRS
            place = block * BLOCK * HEADS + side * HEADS + head
            parts.append(wide(rows_ref, pl.ds(place, PAIRS, stride=2 * HEADS)))
        lefts.append(jnp.concatenate(parts, axis=0).astype(BF16))
        rights.append(jnp.where(heads == head, weight, jnp.zeros_like(weight)))
    return nn(jnp.concatenate(lefts, axis=1), jnp.concatenate(rights, axis=0))


def half_max(value, low_half):
    low = jnp.max(jnp.where(low_half, value, -jnp.inf), axis=1, keepdims=True)
    high = jnp.max(jnp.where(low_half, -jnp.inf, value), axis=1, keepdims=True)
    return jnp.where(low_half, low, high)


def fetch(source, buffer, semaphores, step, first=0):
    slot = lax.rem(step, 2)
    rows = source.shape[1]
    return pltpu.make_async_copy(
        source.at[step], buffer.at[slot, pl.ds(first, rows)], semaphores.at[slot]
    )


def fetch_next(source, buffer, semaphores, step, steps, first=0):
    @pl.when(step + 1 < steps)
    def _():
        fetch(source, buffer, semaphores, step + 1, first).start()

    fetch(source, buffer, semaphores, step, first).wait()
    return buffer.at[lax.rem(step, 2)]


def write_onehot(relative_ref, window, out_ref):
    relative = relative_ref[...].astype(BF16)
    one, zero = jnp.ones((), BF16), jnp.zeros((), BF16)
    place = lax.broadcasted_iota(jnp.int32, (16, LANES), 0).astype(F32)
    for first in range(0, PAIRS, 8):
        rows = [
            jnp.broadcast_to(relative[pair : pair + 1, :], (16, LANES))
            for pair in range(first, first + 8)
        ]
        for row in range(0, window, 16):
            here = (place + float(row)).astype(BF16)
            for pair, wanted in enumerate(rows, first):
                out_ref[row : row + 16, pair * LANES : (pair + 1) * LANES] = jnp.where(
                    here == wanted, one, zero
                )


def diagonal(tile, low_half, less=None):
    parts = []
    for side in range(2):
        lanes = slice(side * LANES, (side + 1) * LANES)
        rows = [slice(side * 16 + part * 8, side * 16 + part * 8 + 8) for part in range(2)]
        both = [tile[row, lanes] if less is None else tile[row, lanes] - less[row] for row in rows]
        parts.append(jnp.where(low_half, both[0], both[1]))
    return parts


def block_rows(value, low_half):
    zero = jnp.zeros_like(value)
    return jnp.concatenate(
        [jnp.where(low_half, value, zero), jnp.where(low_half, zero, value)], axis=0
    ).astype(BF16)


def pack_kernel(
    index_ref,
    rbf_ref,
    query_ref,
    key_ref,
    value_ref,
    out_ref,
    gate_ref,
    up_ref,
    down_ref,
    attn_ref,
    ffn_ref,
    read_ref,
    features_ref,
    small_ref,
    large_ref,
    initial_ref,
    final_ref,
):
    initial_ref[...] = features_ref[:HALO, :]
    final_ref[...] = features_ref[features_ref.shape[0] - HALO :, :]
    shard, width = rbf_ref.shape
    quarter = query_ref.shape[0]
    after_rbf = round_up(shard, 16)
    rest = jnp.zeros((after_rbf - shard, width), F32)
    small_ref[:after_rbf, :] = jnp.concatenate([rbf_ref[...].astype(F32), rest], 0).astype(BF16)
    row = after_rbf
    for ref in (query_ref, key_ref, value_ref):
        small_ref[row : row + quarter, :] = ref[...]
        row += quarter
    vectors = jnp.concatenate([ref[...].astype(F32) for ref in (attn_ref, ffn_ref, read_ref)], 0)
    copies = jnp.concatenate([vectors] * (width // quarter), axis=1)
    owner = lax.broadcasted_iota(jnp.int32, (1, width), 1) // quarter
    own = jnp.where(owner == index_ref[0], copies, 0.0)
    small_ref[row : row + 16, :] = jnp.concatenate(
        [own, jnp.zeros((16 - own.shape[0], width), F32)], 0
    ).astype(BF16)
    row = 0
    for ref in (gate_ref, up_ref):
        for part in range(ref.shape[1] // width):
            large_ref[row : row + quarter, :] = ref[:, part * width : (part + 1) * width]
            row += quarter
    for ref in (down_ref, out_ref):
        large_ref[row : row + ref.shape[0], :] = ref[...]
        row += ref.shape[0]


def pack_call(index, rbf, query, key, value, out, gate, up, down, *rest):
    width = rbf.shape[1]
    quarter = query.shape[0]
    vmem = pl.BlockSpec(memory_space=pltpu.VMEM)
    small = round_up(rbf.shape[0], 16) + 3 * quarter + 16
    large = 2 * quarter * (gate.shape[1] // width) + down.shape[0] + quarter
    return pl.pallas_call(
        pack_kernel,
        out_shape=(
            jax.ShapeDtypeStruct((small, width), BF16),
            jax.ShapeDtypeStruct((large, width), BF16),
            jax.ShapeDtypeStruct((HALO, width), BF16),
            jax.ShapeDtypeStruct((HALO, width), BF16),
        ),
        in_specs=[pl.BlockSpec(memory_space=pltpu.SMEM)] + [vmem] * 12,
        out_specs=(vmem,) * 4,
        cost_estimate=pl.CostEstimate(flops=0, bytes_accessed=2**21, transcendentals=0),
        name="pack_weights",
    )(index, rbf, query, key, value, out, gate, up, down, *rest)


def basis_kernel(
    shard, padded, spread, step, dist_ref, rows_ref, out_ref, relative_ref, by_atom, scaled, envelopes
):
    block = pl.program_id(0)
    factor = math.sqrt(0.5 / math.log(2.0)) / spread

    @pl.when(block == 0)
    def _():
        by_atom[0] = dist_ref[...].T
        by_atom[1] = rows_ref[...].astype(F32).T

    place = pl.ds(pl.multiple_of(block * BLOCK, BLOCK), BLOCK)
    dist = pair_rows(by_atom[0, place, :])
    scaled[...] = dist * factor
    envelopes[...] = 0.5 * (jnp.cos(jnp.pi * dist / CUTOFF) + 1.0)
    relative_ref[...] = pair_rows(by_atom[1, place, :]) - (block * BLOCK).astype(F32)
    rows = out_ref.shape[0]
    iota = lax.broadcasted_iota(jnp.int32, (8, LANES), 0).astype(F32) * (step * factor)
    center = lambda row: ((row // padded) * shard + row % padded) * step * factor

    for first in range(0, PAIRS, 8):
        pairs = range(first, first + 8)
        bases = [scaled[pair : pair + 1, :] - iota for pair in pairs]
        heights = [jnp.broadcast_to(envelopes[pair : pair + 1, :], (16, LANES)) for pair in pairs]
        for row in range(0, rows, 16):
            for pair, base, height in zip(pairs, bases, heights):
                delta = jnp.concatenate([base - center(row), base - center(row + 8)], axis=0)
                value = jnp.exp2(-(delta * delta)) * height
                out_ref[row : row + 16, pair * LANES : (pair + 1) * LANES] = value.astype(BF16)


def basis_call(distances, neighbours, shard, padded, members, basis_count):
    slots, atoms = distances.shape
    blocks = atoms // BLOCK
    rows = members * padded
    edges = BLOCK * slots
    whole = pl.BlockSpec((slots, atoms), lambda b: (0, 0))
    return pl.pallas_call(
        functools.partial(
            basis_kernel, shard, padded, 2.0 * CUTOFF / basis_count, CUTOFF / basis_count
        ),
        grid=(blocks,),
        out_shape=(
            jax.ShapeDtypeStruct((blocks, rows, edges), BF16),
            jax.ShapeDtypeStruct((blocks, PAIRS, LANES), F32),
        ),
        in_specs=[whole, whole],
        out_specs=(
            pl.BlockSpec((None, rows, edges), lambda b: (b, 0, 0)),
            pl.BlockSpec((None, PAIRS, LANES), lambda b: (b, 0, 0)),
        ),
        scratch_shapes=[
            pltpu.VMEM((2, atoms, slots), F32),
            pltpu.VMEM((PAIRS, LANES), F32),
            pltpu.VMEM((PAIRS, LANES), F32),
        ],
        compiler_params=pltpu.CompilerParams(vmem_limit_bytes=40 * 2**20),
        cost_estimate=pl.CostEstimate(
            flops=8 * atoms * slots * rows,
            bytes_accessed=2 * atoms * slots * rows,
            transcendentals=atoms * slots * rows,
        ),
        name="radial_basis",
    )(distances, neighbours)


def place_shards(index_ref, packs, row, count, out_ref):
    me = index_ref[0]
    for offset, pack in enumerate(packs):
        owner = lax.bitwise_xor(me, offset)
        start = pl.multiple_of(owner * count, 8)
        out_ref[pl.ds(start, count), :] = pack[row : row + count, :].astype(out_ref.dtype)


def vector_of(packs, row):
    total = packs[0][row : row + 1, :].astype(F32)
    for pack in packs[1:]:
        total = total + pack[row : row + 1, :].astype(F32)
    return total


def forward_kernel(
    padded,
    quarter,
    scale,
    index_ref,
    counts_ref,
    features_ref,
    before_ref,
    after_ref,
    pack0,
    pack1,
    pack2,
    pack3,
    relative_ref,
    basis_hbm,
    edge_ref,
    power_ref,
    inverse_ref,
    pooled_ref,
    attended_ref,
    lookup_ref,
    query_ref,
    kvq_ref,
    weight_t,
    assembled,
    spread,
    keyed,
    bands,
    pooled,
    phi_buffer,
    semaphores,
):
    step = pl.program_id(0)
    steps = pl.num_programs(0)
    packs = (pack0, pack1, pack2, pack3)
    atoms, width = features_ref.shape
    low_half = lax.broadcasted_iota(jnp.int32, (1, LANES), 1) < LANES // 2
    lane = lax.broadcasted_iota(jnp.int32, (1, LANES), 1)
    edges = edge_ref.shape[1]
    window = BLOCK + 2 * HALO

    @pl.when(step == 0)
    def _():
        fetch(basis_hbm, phi_buffer, semaphores, 0, window).start()
        place_shards(index_ref, packs, 0, padded, assembled)
        weight_t[:, window:] = assembled[...].T.astype(BF16)
        start = round_up(padded, 16)
        for which in range(3):
            place_shards(index_ref, packs, start + which * quarter, quarter, kvq_ref.at[which])
        gain = vector_of(packs, start + 3 * quarter)
        for ref, start in ((before_ref, 0), (features_ref, HALO), (after_ref, HALO + atoms)):
            normed, _ = rms(ref[...].astype(F32))
            lookup_ref[start : start + ref.shape[0], :] = (normed * gain).astype(BF16)
        query = nn(lookup_ref[HALO : HALO + atoms, :], kvq_ref[0]).astype(BF16)
        query_ref[...] = query
        spread_heads(query.astype(F32), spread)
        keyed[...] = (nt(wide(spread).astype(BF16), kvq_ref[1]) * scale).astype(BF16)
        bands[...] = jnp.zeros_like(bands)

    table = lookup_ref[pl.ds(pl.multiple_of(step * BLOCK, BLOCK), window), :]
    weight_t[:, :window] = table.astype(F32).T.astype(BF16)
    phi = phi_buffer.at[lax.rem(step, 2)]
    write_onehot(relative_ref, window, phi)
    fetch_next(basis_hbm, phi_buffer, semaphores, step, steps, window)
    wide_part = 2 * GROUP
    for start in range(0, edges, wide_part):
        part = slice(start, start + wide_part)
        edge_ref[:, part] = nn(weight_t[...], phi[:, part]).astype(BF16)
    rows = BLOCK * HEADS
    base = pl.multiple_of(step * rows, rows)
    scores = []
    for tile in range(edges // TILE):
        left = keyed[pl.ds(base + tile * 32, 32), :]
        right = edge_ref[:, tile * TILE : (tile + 1) * TILE]
        for side, score in enumerate(diagonal(nn(left, right), low_half)):
            pair = 2 * tile + side
            low_count = counts_ref[step * BLOCK + pair]
            high_count = counts_ref[step * BLOCK + PAIRS + pair]
            usable = lane < jnp.where(low_half, low_count, high_count + LANES // 2)
            scores.append(jnp.where(usable, score, -1e30))
    score = jnp.concatenate(scores, axis=0)
    power = jnp.exp(score - half_max(score, low_half))
    power_ref[...] = power.astype(BF16)
    group_rows = bands.shape[1]
    pairs = GROUP // LANES
    ones = jnp.ones((GROUP, LANES), BF16)
    for pair in range(PAIRS):
        group, place = pair // pairs, pair % pairs
        bands[
            group, place * 16 : (place + 1) * 16, place * LANES : (place + 1) * LANES
        ] = block_rows(power[pair * 8 : (pair + 1) * 8], low_half)
    for group in range(edges // GROUP):
        part = slice(group * GROUP, (group + 1) * GROUP)
        band = bands[group]
        inverse = 1.0 / nn(band, ones)
        result = nt(band, edge_ref[:, part])
        rows = slice(group * group_rows, (group + 1) * group_rows)
        place = pl.ds(base + group * group_rows, group_rows)
        inverse_ref[rows, :] = inverse
        for half in range(width // LANES):
            lanes = slice(half * LANES, (half + 1) * LANES)
            value = result[:, lanes] * inverse
            pooled[half, place, :] = value
            pooled_ref[rows, lanes] = value.astype(BF16)

    @pl.when(step == steps - 1)
    def _():
        attended_ref[...] = gather_heads(pooled, kvq_ref[2], atoms).astype(BF16)


def forward_call(index, counts, features, before, after, packs, relative, basis, padded, quarter):
    atoms, width = features.shape
    blocks, rows, edges = basis.shape
    slots = edges // BLOCK
    table = atoms + 2 * HALO
    full = lambda shape: pl.BlockSpec(shape, lambda b: (0,) * len(shape))
    head_rows = atoms * HEADS
    window = BLOCK + 2 * HALO
    group_rows = GROUP // slots * HEADS
    return pl.pallas_call(
        functools.partial(forward_kernel, padded, quarter, (width // HEADS) ** -0.5),
        grid=(blocks,),
        out_shape=(
            jax.ShapeDtypeStruct((blocks, width, edges), BF16),
            jax.ShapeDtypeStruct((blocks, PAIRS * HEADS, LANES), BF16),
            jax.ShapeDtypeStruct((head_rows, LANES), F32),
            jax.ShapeDtypeStruct((head_rows, width), BF16),
            jax.ShapeDtypeStruct((atoms, width), BF16),
            jax.ShapeDtypeStruct((table, width), BF16),
            jax.ShapeDtypeStruct((atoms, width), BF16),
            jax.ShapeDtypeStruct((3, width, width), BF16),
        ),
        in_specs=[
            pl.BlockSpec(memory_space=pltpu.SMEM),
            pl.BlockSpec(memory_space=pltpu.SMEM),
            full((atoms, width)),
            full((HALO, width)),
            full((HALO, width)),
        ]
        + [full(pack.shape) for pack in packs]
        + [
            pl.BlockSpec((None, PAIRS, LANES), lambda b: (b, 0, 0)),
            pl.BlockSpec(memory_space=pl.ANY),
        ],
        out_specs=(
            pl.BlockSpec((None, width, edges), lambda b: (b, 0, 0)),
            pl.BlockSpec((None, PAIRS * HEADS, LANES), lambda b: (b, 0, 0)),
            pl.BlockSpec((BLOCK * HEADS, LANES), lambda b: (b, 0)),
            pl.BlockSpec((BLOCK * HEADS, width), lambda b: (b, 0)),
            full((atoms, width)),
            full((table, width)),
            full((atoms, width)),
            full((3, width, width)),
        ),
        scratch_shapes=[
            pltpu.VMEM((width, window + rows), BF16),
            pltpu.VMEM((rows, width), F32),
            pltpu.VMEM((width // LANES, head_rows, LANES), F32),
            pltpu.VMEM((head_rows, width), BF16),
            pltpu.VMEM((edges // GROUP, group_rows, GROUP), BF16),
            pltpu.VMEM((width // LANES, head_rows, LANES), F32),
            pltpu.VMEM((2, window + rows, edges), BF16),
            pltpu.SemaphoreType.DMA((2,)),
        ],
        compiler_params=pltpu.CompilerParams(vmem_limit_bytes=58 * 2**20),
        cost_estimate=pl.CostEstimate(
            flops=2 * atoms * slots * width * (rows + window + 64),
            bytes_accessed=2 * atoms * slots * (rows + width),
            transcendentals=atoms * slots * HEADS,
        ),
        name="attention_forward",
    )(index, counts, features, before, after, *packs, relative, basis)


def ffn_kernel(
    quarter,
    small_row,
    index_ref,
    features_ref,
    attended_ref,
    grad_out_ref,
    grad_energy_ref,
    small0,
    small1,
    small2,
    small3,
    pack0,
    pack1,
    pack2,
    pack3,
    out_ref,
    energy_ref,
    grad_residual_ref,
    grad_attended_ref,
    sums_ref,
    grads0,
    grads1,
    grads2,
    grads3,
    w_gate,
    w_up,
    w_down,
    w_out,
    g_gate,
    g_up,
    g_down,
    g_out,
):
    small = (small0, small1, small2, small3)
    packs = (pack0, pack1, pack2, pack3)
    atoms, width = features_ref.shape
    parts = w_gate.shape[1] // width
    down_rows = w_down.shape[0] // 4
    me = index_ref[0]
    for offset, pack in enumerate(packs):
        owner = lax.bitwise_xor(me, offset)
        rows = pl.ds(pl.multiple_of(owner * quarter, 16), quarter)
        for part in range(parts):
            lanes = slice(part * width, (part + 1) * width)
            w_gate[rows, lanes] = pack[part * quarter : (part + 1) * quarter, :]
            w_up[rows, lanes] = pack[(parts + part) * quarter : (parts + part + 1) * quarter, :]
        start = 2 * parts * quarter
        w_down[pl.ds(pl.multiple_of(owner * down_rows, 16), down_rows), :] = pack[
            start : start + down_rows, :
        ]
        w_out[rows, :] = pack[start + down_rows : start + down_rows + quarter, :]
    gain = vector_of(small, small_row + 1)
    readout = vector_of(small, small_row + 2)

    attended = attended_ref[...]
    residual = features_ref[...].astype(F32) + nn(attended, w_out[...])
    normed, inverse = rms(residual)
    hidden = (normed * gain).astype(BF16)
    gate = nn(hidden, w_gate[...])
    up = nn(hidden, w_up[...])
    sigmoid = jax.nn.sigmoid(gate)
    silu = gate * sigmoid
    activated = (silu * up).astype(BF16)
    outputs = residual + nn(activated, w_down[...])
    out_ref[...] = outputs
    energy = jnp.sum(outputs * readout, -1, keepdims=True)
    energy_ref[...] = jnp.broadcast_to(energy, (atoms, LANES)).T[:1, :]
    grad_energy = jnp.broadcast_to(grad_energy_ref[...], (LANES, atoms)).T[:, :1]
    grad_act = grad_out_ref[...].astype(F32) + grad_energy * readout
    grad_branch = grad_act.astype(BF16)
    g_down[...] = tn(activated, grad_branch)
    grad_activated = nt(grad_branch, w_down[...])
    grad_gate = (grad_activated * up * sigmoid * (1.0 + gate * (1.0 - sigmoid))).astype(BF16)
    grad_up = (grad_activated * silu).astype(BF16)
    g_gate[...] = tn(hidden, grad_gate)
    g_up[...] = tn(hidden, grad_up)
    grad_hidden = (nt(grad_gate, w_gate[...]) + nt(grad_up, w_up[...])).astype(BF16).astype(F32)
    grad_residual = grad_act + norm_back(grad_hidden * gain, normed, inverse)
    grad_residual_ref[...] = grad_residual
    grad_proj = grad_residual.astype(BF16)
    grad_attended_ref[...] = nt(grad_proj, w_out[...]).astype(BF16)
    g_out[...] = tn(attended, grad_proj)
    for offset, grads in enumerate((grads0, grads1, grads2, grads3)):
        owner = lax.bitwise_xor(me, offset)
        rows = pl.ds(pl.multiple_of(owner * quarter, 16), quarter)
        row = 0
        for grad in (g_gate, g_up):
            for part in range(parts):
                lanes = slice(part * width, (part + 1) * width)
                grads[row : row + quarter, :] = grad[rows, lanes].astype(BF16)
                row += quarter
        down = pl.ds(pl.multiple_of(owner * down_rows, 16), down_rows)
        grads[row : row + down_rows, :] = g_down[down, :].astype(BF16)
        row += down_rows
        grads[row : row + quarter, :] = g_out[rows, :].astype(BF16)
    sums_ref[...] = jnp.zeros_like(sums_ref)
    sums_ref[1:2, :] = jnp.sum(grad_hidden * normed, 0, keepdims=True)
    sums_ref[2:3, :] = jnp.sum(grad_energy * outputs, 0, keepdims=True)


def ffn_call(index, features, attended, grad_out, grad_energy, small, packs, hidden, quarter, row):
    atoms, width = features.shape
    vmem = pl.BlockSpec(memory_space=pltpu.VMEM)
    return pl.pallas_call(
        functools.partial(ffn_kernel, quarter, row),
        out_shape=(
            jax.ShapeDtypeStruct((atoms, width), F32),
            jax.ShapeDtypeStruct((1, atoms), F32),
            jax.ShapeDtypeStruct((atoms, width), F32),
            jax.ShapeDtypeStruct((atoms, width), BF16),
            jax.ShapeDtypeStruct((8, width), F32),
        )
        + (jax.ShapeDtypeStruct(packs[0].shape, BF16),) * 4,
        in_specs=[pl.BlockSpec(memory_space=pltpu.SMEM)] + [vmem] * 12,
        out_specs=(vmem,) * 9,
        scratch_shapes=[
            pltpu.VMEM(shape, dtype)
            for dtype in (BF16, F32)
            for shape in ((width, hidden), (width, hidden), (hidden, width), (width, width))
        ],
        compiler_params=pltpu.CompilerParams(vmem_limit_bytes=58 * 2**20),
        cost_estimate=pl.CostEstimate(
            flops=18 * atoms * width * hidden, bytes_accessed=2**23, transcendentals=atoms * hidden
        ),
        name="feed_forward",
    )(index, features, attended, grad_out, grad_energy, *small, *packs)


def score_kernel(
    quarter,
    scale,
    index_ref,
    lookup_ref,
    query_ref,
    kvq_ref,
    pooled_ref,
    inverse_ref,
    attended_ref,
    grad_attended_ref,
    power_ref,
    edge_ref,
    grad_score_ref,
    mixed_ref,
    grad_query_ref,
    grads0,
    grads1,
    grads2,
    grads3,
    spread_q,
    spread_g,
    scaled,
    valued,
    means,
    bands,
    pooled,
    weight_grad,
):
    step = pl.program_id(0)
    atoms, width = query_ref.shape
    low_half = lax.broadcasted_iota(jnp.int32, (1, LANES), 1) < LANES // 2
    edges = edge_ref.shape[1]
    group_rows = bands.shape[1]
    groups = edges // GROUP
    pairs = GROUP // LANES

    @pl.when(step == 0)
    def _():
        grad_attended = grad_attended_ref[...].astype(F32)
        product = grad_attended * attended_ref[...].astype(F32)
        high = product.astype(BF16)
        low = (product - high.astype(F32)).astype(BF16)
        heads = lax.broadcasted_iota(jnp.int32, (width, HEADS * LANES), 0) // (width // HEADS)
        copies = lax.broadcasted_iota(jnp.int32, (width, HEADS * LANES), 1) // LANES
        summing = jnp.where(heads == copies, 1.0, 0.0).astype(BF16)
        mean = nn(high, summing) + nn(low, summing)
        for start in range(0, atoms, PAIRS):
            block, side = start // BLOCK, (start % BLOCK) // PAIRS
            for head in range(HEADS):
                place = block * BLOCK * HEADS + side * HEADS + head
                means[pl.ds(place, PAIRS, stride=2 * HEADS), :] = mean[
                    start : start + PAIRS, head * LANES : (head + 1) * LANES
                ]
        inverse = inverse_ref[...]
        means[...] = means[...] * inverse
        spread_heads(query_ref[...].astype(F32), pooled)
        spread_q[...] = wide(pooled).astype(BF16)
        spread_heads(grad_attended, pooled)
        spread_g[...] = wide(pooled).astype(BF16)
        scaled[...] = (wide(pooled) * jnp.concatenate([inverse] * (width // LANES), axis=1)).astype(
            BF16
        )
        valued[...] = nt(scaled[...], kvq_ref[2]).astype(BF16)
        bands[...] = jnp.zeros_like(bands)

    rows = BLOCK * HEADS
    base = pl.multiple_of(step * rows, rows)
    for group in range(groups):
        place = pl.ds(base + group * group_rows, group_rows)
        mixed_ref[group, :, :group_rows] = (nt(kvq_ref[1], spread_q[place, :]) * scale).astype(BF16)
        mixed_ref[group, :, group_rows:] = nt(kvq_ref[2], scaled[place, :]).astype(BF16)
    power = power_ref[...].astype(F32)
    for tile in range(edges // TILE):
        place = pl.ds(base + tile * 32, 32)
        product = nn(valued[place, :], edge_ref[:, tile * TILE : (tile + 1) * TILE])
        for side, grad_soft in enumerate(diagonal(product, low_half, means[place, :])):
            pair = 2 * tile + side
            own = slice(pair * 8, (pair + 1) * 8)
            group, column = pair // pairs, pair % pairs
            value = power[own] * grad_soft
            grad_score_ref[own, :] = value
            bands[
                group, column * 16 : (column + 1) * 16, column * LANES : (column + 1) * LANES
            ] = block_rows(value, low_half)
    for group in range(groups):
        result = nt(bands[group], edge_ref[:, group * GROUP : (group + 1) * GROUP])
        for half in range(width // LANES):
            pooled[half, pl.ds(base + group * group_rows, group_rows), :] = result[
                :, half * LANES : (half + 1) * LANES
            ]

    @pl.when(step == pl.num_programs(0) - 1)
    def _():
        grad_query = (gather_heads(pooled, kvq_ref[1], atoms) * scale).astype(BF16)
        grad_query_ref[...] = grad_query
        weight_grad[0] = tn(lookup_ref[HALO : HALO + atoms, :], grad_query)
        weight_grad[1] = tn(wide(pooled).astype(BF16), spread_q[...]) * scale
        weight_grad[2] = tn(pooled_ref[...], spread_g[...])
        me = index_ref[0]
        for offset, grads in enumerate((grads0, grads1, grads2, grads3)):
            owner = lax.bitwise_xor(me, offset)
            rows = pl.ds(pl.multiple_of(owner * quarter, 16), quarter)
            for which in range(3):
                grads[which * quarter : (which + 1) * quarter, :] = weight_grad[
                    which, rows, :
                ].astype(BF16)


def score_call(
    index, lookup, query, kvq, pooled, inverse, attended, grad_attended, power, edge, quarter
):
    atoms, width = query.shape
    blocks, _, edges = edge.shape
    head_rows = atoms * HEADS
    group_rows = GROUP // (edges // BLOCK) * HEADS
    groups = edges // GROUP
    full = lambda shape: pl.BlockSpec(shape, lambda b: (0,) * len(shape))
    whole = (lookup, query, kvq, pooled, inverse, attended, grad_attended)
    pair_block = pl.BlockSpec((None, PAIRS * HEADS, LANES), lambda b: (b, 0, 0))
    grads = (3 * quarter, width)
    return pl.pallas_call(
        functools.partial(score_kernel, quarter, (width // HEADS) ** -0.5),
        grid=(blocks,),
        out_shape=(
            jax.ShapeDtypeStruct((blocks, PAIRS * HEADS, LANES), F32),
            jax.ShapeDtypeStruct((blocks * groups, width, 2 * group_rows), BF16),
            jax.ShapeDtypeStruct((atoms, width), BF16),
        )
        + (jax.ShapeDtypeStruct(grads, BF16),) * 4,
        in_specs=[pl.BlockSpec(memory_space=pltpu.SMEM)]
        + [full(value.shape) for value in whole]
        + [pair_block, pl.BlockSpec((None, width, edges), lambda b: (b, 0, 0))],
        out_specs=(
            pair_block,
            pl.BlockSpec((groups, width, 2 * group_rows), lambda b: (b, 0, 0)),
            full((atoms, width)),
        )
        + (full(grads),) * 4,
        scratch_shapes=[
            pltpu.VMEM((head_rows, width), BF16),
            pltpu.VMEM((head_rows, width), BF16),
            pltpu.VMEM((head_rows, width), BF16),
            pltpu.VMEM((head_rows, width), BF16),
            pltpu.VMEM((head_rows, LANES), F32),
            pltpu.VMEM((groups, group_rows, GROUP), BF16),
            pltpu.VMEM((width // LANES, head_rows, LANES), F32),
            pltpu.VMEM((3, width, width), F32),
        ],
        compiler_params=pltpu.CompilerParams(vmem_limit_bytes=58 * 2**20),
        cost_estimate=pl.CostEstimate(
            flops=2 * atoms * edges // BLOCK * width * 256,
            bytes_accessed=2 * blocks * width * edges,
            transcendentals=0,
        ),
        name="score_backward",
    )(index, *whole, power, edge)


def edge_kernel(padded, gain_row, first_block, last_block, carried, final, *refs):
    refs = list(refs)
    take = lambda count: [refs.pop(0) for _ in range(count)]
    relative_ref, power_ref, grad_score_ref, mixed_ref, basis_hbm = take(5)
    before = take(2 if carried else 0)
    if final:
        index_ref, features_ref, before_ref, after_ref, grad_query_ref, kvq_ref = take(6)
        grad_residual_ref, sums_ref = take(2)
        small = take(4)
        grad_own_ref, grad_lower_ref, grad_upper_ref = take(3)
        grads_refs = take(4)
    grad_rbf, grad_lookup = take(2)
    bands, grad_edge, phi_buffer, semaphores = take(4)
    block = pl.program_id(0) + first_block
    width, edges = grad_edge.shape
    window = BLOCK + 2 * HALO
    low_half = lax.broadcasted_iota(jnp.int32, (1, LANES), 1) < LANES // 2
    group_rows = bands.shape[1] // 2
    groups = edges // GROUP
    pairs = GROUP // LANES

    @pl.when(block == first_block)
    def _():
        fetch(basis_hbm, phi_buffer, semaphores, block, window).start()
        bands[...] = jnp.zeros_like(bands)
        if carried:
            grad_rbf[...] = before[0][...]
            grad_lookup[...] = before[1][...]
        else:
            grad_rbf[...] = jnp.zeros_like(grad_rbf)
            grad_lookup[...] = jnp.zeros_like(grad_lookup)

    power = power_ref[...].astype(F32)
    grad_score = grad_score_ref[...]
    for pair in range(PAIRS):
        group, column = pair // pairs, pair % pairs
        own = slice(pair * 8, (pair + 1) * 8)
        lanes = slice(column * LANES, (column + 1) * LANES)
        for start, value in ((0, grad_score[own]), (group_rows, power[own])):
            row = start + column * 16
            bands[group, row : row + 16, lanes] = block_rows(value, low_half)
    for group in range(groups):
        part = slice(group * GROUP, (group + 1) * GROUP)
        grad_edge[:, part] = nn(mixed_ref[group], bands[group]).astype(BF16)
    phi = phi_buffer.at[lax.rem(block, 2)]
    write_onehot(relative_ref, window, phi)
    fetch_next(basis_hbm, phi_buffer, semaphores, block, last_block, window)
    total = nt(phi[...], grad_edge[...])
    grad_lookup[pl.ds(pl.multiple_of(block * BLOCK, BLOCK), window), :] += total[:window]
    grad_rbf[...] += total[window:]

    if not final:
        return

    @pl.when(block == last_block - 1)
    def _():
        atoms = features_ref.shape[0]
        grad_lookup[HALO : HALO + atoms, :] += nt(grad_query_ref[...], kvq_ref[0])
        gain = vector_of(small, gain_row)
        grad_gain = jnp.zeros((1, width), F32)
        places = (
            (before_ref, 0, grad_lower_ref),
            (features_ref, HALO, grad_own_ref),
            (after_ref, HALO + atoms, grad_upper_ref),
        )
        for ref, start, out in places:
            normed, inverse = rms(ref[...].astype(F32))
            grad = grad_lookup[start : start + ref.shape[0], :]
            grad_gain = grad_gain + jnp.sum(grad * normed, 0, keepdims=True)
            back = norm_back(grad * gain, normed, inverse)
            if start == HALO:
                back = back + grad_residual_ref[...]
            out[...] = back.astype(out.dtype)
        vectors = jnp.concatenate([grad_gain, sums_ref[1:8, :], jnp.zeros((8, width), F32)], 0)
        after_rbf = round_up(padded, 16)
        rest = jnp.zeros((after_rbf - padded, width), F32)
        me = index_ref[0]
        for offset, grads in enumerate(grads_refs):
            owner = lax.bitwise_xor(me, offset)
            rbf = grad_rbf[pl.ds(pl.multiple_of(owner * padded, 8), padded), :]
            grads[:after_rbf, :] = jnp.concatenate([rbf, rest], 0).astype(BF16)
            grads[after_rbf:, :] = vectors.astype(BF16)


def edge_call(arrays, basis, carry, last, padded, gain_row, first_block, last_block):
    blocks, rows, edges = basis.shape
    width = arrays[3].shape[1]
    groups = edges // GROUP
    group_rows = GROUP // (edges // BLOCK) * HEADS
    table = blocks * BLOCK + 2 * HALO
    window = BLOCK + 2 * HALO
    full = lambda shape: pl.BlockSpec(shape, lambda b: (0,) * len(shape))
    here = lambda b: (b + first_block, 0, 0)
    in_specs = [
        pl.BlockSpec((None, PAIRS, LANES), here),
        pl.BlockSpec((None, PAIRS * HEADS, LANES), here),
        pl.BlockSpec((None, PAIRS * HEADS, LANES), here),
        pl.BlockSpec((groups, width, 2 * group_rows), here),
        pl.BlockSpec(memory_space=pl.ANY),
    ]
    operands = [*arrays, basis]
    sums = [(rows, width), (table, width)]
    if carry is not None:
        in_specs += [full(value.shape) for value in carry]
        operands += list(carry)
    scratch = [
        pltpu.VMEM((groups, 2 * group_rows, GROUP), BF16),
        pltpu.VMEM((width, edges), BF16),
        pltpu.VMEM((2, window + rows, edges), BF16),
        pltpu.SemaphoreType.DMA((2,)),
    ]
    if last is None:
        shapes = [(shape, F32) for shape in sums]
    else:
        in_specs += [pl.BlockSpec(memory_space=pltpu.SMEM)]
        in_specs += [full(value.shape) for value in last[1:]]
        operands += list(last)
        grads = (round_up(padded, 16) + 16, width)
        shapes = [((blocks * BLOCK, width), F32)] + [((HALO, width), BF16)] * 2 + [(grads, BF16)] * 4
        scratch = [pltpu.VMEM(shape, F32) for shape in sums] + scratch
    return pl.pallas_call(
        functools.partial(
            edge_kernel, padded, gain_row, first_block, last_block, carry is not None, last is not None
        ),
        grid=(last_block - first_block,),
        out_shape=[jax.ShapeDtypeStruct(shape, dtype) for shape, dtype in shapes],
        in_specs=in_specs,
        out_specs=[full(shape) for shape, _ in shapes],
        scratch_shapes=scratch,
        compiler_params=pltpu.CompilerParams(vmem_limit_bytes=58 * 2**20),
        cost_estimate=pl.CostEstimate(
            flops=2 * (last_block - first_block) * edges * width * (rows + window + 256),
            bytes_accessed=2 * (last_block - first_block) * rows * edges,
            transcendentals=0,
        ),
        name="edge_backward",
    )(*operands)


def large_kernel(first, second, gate, up, down, out):
    total = lambda rows: first[rows, :].astype(F32) + second[rows, :].astype(F32)
    quarter, width = out.shape
    row = 0
    for ref in (gate, up):
        for part in range(ref.shape[1] // width):
            ref[:, part * width : (part + 1) * width] = total(slice(row, row + quarter))
            row += quarter
    for ref in (down, out):
        ref[...] = total(slice(row, row + ref.shape[0]))
        row += ref.shape[0]


def large_call(first, second, quarter, hidden, down_rows):
    width = first.shape[1]
    vmem = pl.BlockSpec(memory_space=pltpu.VMEM)
    shapes = ((quarter, hidden), (quarter, hidden), (down_rows, width), (quarter, width))
    return pl.pallas_call(
        large_kernel,
        out_shape=[jax.ShapeDtypeStruct(shape, F32) for shape in shapes],
        in_specs=[vmem] * 2,
        out_specs=[vmem] * 4,
        name="feed_forward_results",
    )(first, second)


def small_kernel(
    index_ref,
    score_first,
    score_second,
    edge_first,
    edge_second,
    grad_own,
    from_lower,
    from_upper,
    rbf,
    query,
    key,
    value,
    gain_attn,
    gain_ffn,
    readout,
    features,
):
    quarter = query.shape[0]
    width = query.shape[1]
    for which, ref in enumerate((query, key, value)):
        rows = slice(which * quarter, (which + 1) * quarter)
        ref[...] = score_first[rows, :].astype(F32) + score_second[rows, :].astype(F32)
    total = edge_first[...].astype(F32) + edge_second[...].astype(F32)
    rbf[...] = total[: rbf.shape[0]]
    start = edge_first.shape[0] - 16
    me = index_ref[0]
    for which, ref in enumerate((gain_attn, gain_ffn, readout)):
        row = total[start + which : start + which + 1]
        picked = jnp.zeros((1, quarter), F32)
        for owner in range(width // quarter):
            piece = row[:, owner * quarter : (owner + 1) * quarter]
            picked = picked + jnp.where(me == owner, piece, 0.0)
        ref[...] = picked
    features[...] = grad_own[...]
    features[:HALO, :] += from_lower[...].astype(F32)
    features[features.shape[0] - HALO :, :] += from_upper[...].astype(F32)


def small_call(index, score, edge, grad_own, from_lower, from_upper, shard, quarter):
    width = grad_own.shape[1]
    vmem = pl.BlockSpec(memory_space=pltpu.VMEM)
    shapes = [(shard, width)] + [(quarter, width)] * 3 + [(1, quarter)] * 3 + [grad_own.shape]
    return pl.pallas_call(
        small_kernel,
        out_shape=[jax.ShapeDtypeStruct(shape, F32) for shape in shapes],
        in_specs=[pl.BlockSpec(memory_space=pltpu.SMEM)] + [vmem] * 7,
        out_specs=[vmem] * 8,
        name="edge_results",
    )(index, *score, *edge, grad_own, from_lower, from_upper)


def exchange(value, axis, offset):
    size = lax.axis_size(axis)
    return lax.ppermute(value, axis, [(i, i ^ offset) for i in range(size)])


def shifted(value, by):
    axes = ("space", "wt")
    size = lax.axis_size(axes)
    pairs = [(i, i + by) for i in range(size) if 0 <= i + by < size]
    return lax.ppermute(value, axes, pairs)


def gathered(value):
    return [value] + [exchange(value, "wt", offset) for offset in range(1, lax.axis_size("wt"))]


def added(*values):
    total = values[0].astype(F32)
    for value in values[1:]:
        total = total + value.astype(F32)
    return total.astype(values[0].dtype)


class Reduction:
    def __init__(self, chunks):
        self.offsets = [1 << bit for bit in range(lax.axis_size("space").bit_length() - 1)]
        self.terms = [chunks[0]] + [
            exchange(chunk, "wt", offset) for offset, chunk in enumerate(chunks[1:], 1)
        ]

    def add(self):
        if self.offsets:
            self.terms = [added(*self.terms)]

    def send(self):
        if self.offsets:
            self.terms.append(exchange(self.terms[0], "space", self.offsets.pop(0)))

    def finish(self):
        while self.offsets:
            self.add()
            self.send()
        return self.terms


def between(reductions, value):
    terms = [reduction.terms for reduction in reductions]
    terms, value = lax.optimization_barrier((terms, value))
    for reduction, own in zip(reductions, terms):
        reduction.terms = list(own)
        reduction.add()
    terms = [reduction.terms for reduction in reductions]
    terms, value = lax.optimization_barrier((terms, value))
    for reduction, own in zip(reductions, terms):
        reduction.terms = list(own)
        reduction.send()
    return value


SPLIT = (2, 2, 2)


def local(
    features,
    distances,
    neighbours,
    counts,
    rbf_weight,
    query_weight,
    key_weight,
    value_weight,
    out_weight,
    gate_weight,
    up_weight,
    down_weight,
    attn_gain,
    ffn_gain,
    readout,
    grad_out,
    grad_energy,
):
    members = lax.axis_size("wt")
    atoms, width = features.shape
    shard = rbf_weight.shape[0]
    padded = round_up(shard, 8)
    gain_row = round_up(shard, 16) + 3 * query_weight.shape[0]
    quarter = query_weight.shape[0]
    hidden = gate_weight.shape[1]
    index = lax.axis_index("wt").astype(jnp.int32)[None]

    small, large, initial, final = pack_call(
        index,
        rbf_weight,
        query_weight,
        key_weight,
        value_weight,
        out_weight,
        gate_weight,
        up_weight,
        down_weight,
        attn_gain[None],
        ffn_gain[None],
        readout[None],
        features,
    )
    small_all = gathered(small)
    before = shifted(final, 1)
    after = shifted(initial, -1)
    basis, relative = basis_call(
        distances.T, neighbours.T, shard, padded, members, members * shard
    )

    large, basis = lax.optimization_barrier((large, basis))
    large_all = gathered(large)

    edge, power, inverse, pooled, attended, lookup, query, kvq = forward_call(
        index, counts, features, before, after, small_all, relative, basis, padded, quarter
    )
    outputs, energy, grad_residual, grad_attended, sums, *large_grads = ffn_call(
        index,
        features,
        attended,
        grad_out,
        grad_energy[None, :],
        small_all,
        large_all,
        hidden,
        quarter,
        gain_row,
    )
    grad_score, mixed, grad_query, *score_grads = score_call(
        index, lookup, query, kvq, pooled, inverse, attended, grad_attended, power, edge, quarter
    )
    large_sum, score_sum = Reduction(large_grads), Reduction(score_grads)
    carry, block = None, 0
    last = (index, features, before, after, grad_query, kvq, grad_residual, sums, *small_all)
    for count in SPLIT:
        if carry is None:
            grad_score = between([large_sum], grad_score)
        else:
            carry = between([large_sum, score_sum], carry)
        final = block + count == basis.shape[0]
        carry = edge_call(
            (relative, power, grad_score, mixed),
            basis,
            carry,
            last if final else None,
            padded,
            gain_row,
            block,
            block + count,
        )
        block += count
    grad_own, grad_lower, grad_upper, *edge_grads = carry
    edge_sum = Reduction(edge_grads)
    from_upper = shifted(grad_lower, -1)
    from_lower = shifted(grad_upper, 1)
    score_sum = score_sum.finish()
    results = large_call(*large_sum.finish(), quarter, hidden, down_weight.shape[0])
    grad_gate, grad_up, grad_down, grad_out_w = between([edge_sum], results)
    edge_sum = edge_sum.finish()
    grad_rbf, grad_q, grad_k, grad_v, grad_attn, grad_ffn, grad_read, grad_features = small_call(
        index, score_sum, edge_sum, grad_own, from_lower, from_upper, shard, quarter
    )
    return (
        outputs,
        energy[0],
        grad_features,
        grad_rbf,
        grad_q,
        grad_k,
        grad_v,
        grad_out_w,
        grad_gate,
        grad_up,
        grad_down,
        grad_attn[0],
        grad_ffn[0],
        grad_read[0],
    )


def solution(mesh):
    rows = P(("space", "wt"), None)
    line = P(("space", "wt"))
    in_specs = (rows, rows, rows, line) + (P("wt", None),) * 8 + (P("wt"),) * 3 + (rows, line)
    out_specs = (rows, line, rows) + (P("wt", None),) * 8 + (P("wt"),) * 3
    return jax.shard_map(local, mesh=mesh, in_specs=in_specs, out_specs=out_specs, check_vma=False)
```

```python
import functools
import math

import jax
import jax.numpy as jnp
from jax import lax
from jax.experimental import pallas as pl
from jax.experimental.pallas import tpu as pltpu
from jax.sharding import PartitionSpec as P

HEADS = 8
HALO = 96
EPSILON = 1e-06
CUTOFF = 6.0

BLOCK = 64
PAIRS = BLOCK // 2
LANES = 128
TILE = 256
GROUP = 1024

BF16 = jnp.bfloat16
F32 = jnp.float32


def nn(a, b):
    return lax.dot_general(a, b, (((1,), (0,)), ((), ())), preferred_element_type=F32)


def nt(a, b):
    return lax.dot_general(a, b, (((1,), (1,)), ((), ())), preferred_element_type=F32)


def tn(a, b):
    return lax.dot_general(a, b, (((0,), (0,)), ((), ())), preferred_element_type=F32)


def round_up(value, step):
    return -(-value // step) * step


def rms(value):
    inverse = lax.rsqrt(jnp.mean(value * value, -1, keepdims=True) + EPSILON)
    return value * inverse, inverse


def norm_back(grad_normed, normed_rows, inverse):
    return inverse * (
        grad_normed - normed_rows * jnp.mean(grad_normed * normed_rows, -1, keepdims=True)
    )


def pair_rows(block):
    return jnp.concatenate([block[:PAIRS], block[PAIRS:]], axis=1)


def head_of_lane(width):
    return lax.broadcasted_iota(jnp.int32, (1, width), 1) // (width // HEADS)


def spread_heads(rows, out_ref):
    atoms, width = rows.shape
    heads = head_of_lane(width)
    for start in range(0, atoms, PAIRS):
        block, side = start // BLOCK, (start % BLOCK) // PAIRS
        part = rows[start : start + PAIRS]
        for head in range(HEADS):
            place = block * BLOCK * HEADS + side * HEADS + head
            kept = jnp.where(heads == head, part, 0.0)
            for half in range(width // LANES):
                out_ref[half, pl.ds(place, PAIRS, stride=2 * HEADS), :] = kept[
                    :, half * LANES : (half + 1) * LANES
                ]


def wide(ref, rows=slice(None)):
    return jnp.concatenate([ref[half, rows, :] for half in range(ref.shape[0])], axis=1)


def gather_heads(rows_ref, weight, atoms):
    heads = head_of_lane(weight.shape[1])
    lefts, rights = [], []
    for head in range(HEADS):
        parts = []
        for start in range(0, atoms, PAIRS):
            block, side = start // BLOCK, (start % BLOCK) // PAIRS
            place = block * BLOCK * HEADS + side * HEADS + head
            parts.append(wide(rows_ref, pl.ds(place, PAIRS, stride=2 * HEADS)))
        lefts.append(jnp.concatenate(parts, axis=0).astype(BF16))
        rights.append(jnp.where(heads == head, weight, jnp.zeros_like(weight)))
    return nn(jnp.concatenate(lefts, axis=1), jnp.concatenate(rights, axis=0))


def half_max(value, low_half):
    low = jnp.max(jnp.where(low_half, value, -jnp.inf), axis=1, keepdims=True)
    high = jnp.max(jnp.where(low_half, -jnp.inf, value), axis=1, keepdims=True)
    return jnp.where(low_half, low, high)


def write_onehot(relative, window, out_ref):
    relative = relative.astype(BF16)
    one, zero = jnp.ones((), BF16), jnp.zeros((), BF16)
    place = lax.broadcasted_iota(jnp.int32, (16, LANES), 0).astype(F32)
    pairs = range(relative.shape[0])
    wanted = [jnp.broadcast_to(relative[pair : pair + 1, :], (16, LANES)) for pair in pairs]
    for row in range(0, window, 16):
        here = (place + float(row)).astype(BF16)
        for pair in pairs:
            out_ref[row : row + 16, pair * LANES : (pair + 1) * LANES] = jnp.where(
                here == wanted[pair], one, zero
            )


def write_basis(scaled, heights, shard, padded, step, window, out_ref):
    iota = lax.broadcasted_iota(jnp.int32, (8, LANES), 0).astype(F32) * step
    center = lambda row: ((row // padded) * shard + row % padded) * step
    pairs = range(scaled.shape[0])
    bases = [scaled[pair : pair + 1, :] - iota for pair in pairs]
    tops = [
        jnp.broadcast_to(heights[pair : pair + 1, :], (16, LANES)).astype(BF16) for pair in pairs
    ]
    for row in range(0, out_ref.shape[0] - window, 16):
        for pair, base, top in zip(pairs, bases, tops):
            delta = jnp.concatenate([base - center(row), base - center(row + 8)], axis=0)
            low = delta.astype(BF16)
            value = jnp.exp2(-(low * low)) * top
            out_ref[window + row : window + row + 16, pair * LANES : (pair + 1) * LANES] = value


def write_group(geometry, group, basis, window, out_ref):
    scaled, heights, relative = (
        ref[group * (GROUP // LANES) : (group + 1) * (GROUP // LANES), :] for ref in geometry
    )
    write_onehot(relative, window, out_ref)
    write_basis(scaled, heights, *basis, window, out_ref)


def diagonal(tile, low_half, less=None):
    parts = []
    for side in range(2):
        lanes = slice(side * LANES, (side + 1) * LANES)
        rows = [slice(side * 16 + part * 8, side * 16 + part * 8 + 8) for part in range(2)]
        both = [tile[row, lanes] if less is None else tile[row, lanes] - less[row] for row in rows]
        parts.append(jnp.where(low_half, both[0], both[1]))
    return parts


def block_rows(value, low_half):
    zero = jnp.zeros_like(value)
    return jnp.concatenate(
        [jnp.where(low_half, value, zero), jnp.where(low_half, zero, value)], axis=0
    ).astype(BF16)


def pack_kernel(
    index_ref,
    rbf_ref,
    query_ref,
    key_ref,
    value_ref,
    out_ref,
    gate_ref,
    up_ref,
    down_ref,
    attn_ref,
    ffn_ref,
    read_ref,
    features_ref,
    small_ref,
    large_ref,
    initial_ref,
    final_ref,
):
    initial_ref[...] = features_ref[:HALO, :]
    final_ref[...] = features_ref[features_ref.shape[0] - HALO :, :]
    shard, width = rbf_ref.shape
    quarter = query_ref.shape[0]
    after_rbf = round_up(shard, 16)
    rest = jnp.zeros((after_rbf - shard, width), F32)
    small_ref[:after_rbf, :] = jnp.concatenate([rbf_ref[...].astype(F32), rest], 0).astype(BF16)
    row = after_rbf
    for ref in (query_ref, key_ref, value_ref):
        small_ref[row : row + quarter, :] = ref[...]
        row += quarter
    vectors = jnp.concatenate([ref[...].astype(F32) for ref in (attn_ref, ffn_ref, read_ref)], 0)
    copies = jnp.concatenate([vectors] * (width // quarter), axis=1)
    owner = lax.broadcasted_iota(jnp.int32, (1, width), 1) // quarter
    own = jnp.where(owner == index_ref[0], copies, 0.0)
    small_ref[row : row + 16, :] = jnp.concatenate(
        [own, jnp.zeros((16 - own.shape[0], width), F32)], 0
    ).astype(BF16)
    row = 0
    for ref in (gate_ref, up_ref):
        for part in range(ref.shape[1] // width):
            large_ref[row : row + quarter, :] = ref[:, part * width : (part + 1) * width]
            row += quarter
    for ref in (down_ref, out_ref):
        large_ref[row : row + ref.shape[0], :] = ref[...]
        row += ref.shape[0]


def pack_call(index, rbf, query, key, value, out, gate, up, down, *rest):
    width = rbf.shape[1]
    quarter = query.shape[0]
    vmem = pl.BlockSpec(memory_space=pltpu.VMEM)
    small = round_up(rbf.shape[0], 16) + 3 * quarter + 16
    large = 2 * quarter * (gate.shape[1] // width) + down.shape[0] + quarter
    return pl.pallas_call(
        pack_kernel,
        out_shape=(
            jax.ShapeDtypeStruct((small, width), BF16),
            jax.ShapeDtypeStruct((large, width), BF16),
            jax.ShapeDtypeStruct((HALO, width), BF16),
            jax.ShapeDtypeStruct((HALO, width), BF16),
        ),
        in_specs=[pl.BlockSpec(memory_space=pltpu.SMEM)] + [vmem] * 12,
        out_specs=(vmem,) * 4,
        cost_estimate=pl.CostEstimate(flops=0, bytes_accessed=2**21, transcendentals=0),
        name="pack_weights",
    )(index, rbf, query, key, value, out, gate, up, down, *rest)


def geometry_kernel(factor, dist_ref, rows_ref, scaled_ref, heights_ref, relative_ref):
    dist = dist_ref[...].T
    rows = rows_ref[...].astype(F32).T
    for block in range(scaled_ref.shape[0]):
        place = slice(block * BLOCK, (block + 1) * BLOCK)
        pairs = pair_rows(dist[place])
        scaled_ref[block] = pairs * factor
        heights_ref[block] = 0.5 * (jnp.cos(jnp.pi * pairs / CUTOFF) + 1.0)
        relative_ref[block] = pair_rows(rows[place]) - float(block * BLOCK)


def geometry_call(distances, neighbours, factor):
    slots, atoms = distances.shape
    blocks = atoms // BLOCK
    vmem = pl.BlockSpec(memory_space=pltpu.VMEM)
    return pl.pallas_call(
        functools.partial(geometry_kernel, factor),
        out_shape=(jax.ShapeDtypeStruct((blocks, PAIRS, LANES), F32),) * 3,
        in_specs=[vmem, vmem],
        out_specs=(vmem,) * 3,
        cost_estimate=pl.CostEstimate(
            flops=40 * atoms * slots, bytes_accessed=20 * atoms * slots, transcendentals=0
        ),
        name="edge_geometry",
    )(distances, neighbours)


def basis_factor(basis_count):
    return math.sqrt(0.5 / math.log(2.0)) * basis_count / (2.0 * CUTOFF)


def place_shards(index_ref, packs, row, count, out_ref):
    me = index_ref[0]
    for offset, pack in enumerate(packs):
        owner = lax.bitwise_xor(me, offset)
        start = pl.multiple_of(owner * count, 8)
        out_ref[pl.ds(start, count), :] = pack[row : row + count, :].astype(out_ref.dtype)


def vector_of(packs, row):
    total = packs[0][row : row + 1, :].astype(F32)
    for pack in packs[1:]:
        total = total + pack[row : row + 1, :].astype(F32)
    return total


def forward_kernel(
    basis,
    quarter,
    scale,
    index_ref,
    counts_ref,
    features_ref,
    before_ref,
    after_ref,
    pack0,
    pack1,
    pack2,
    pack3,
    scaled_ref,
    heights_ref,
    relative_ref,
    edge_ref,
    power_ref,
    inverse_ref,
    pooled_ref,
    attended_ref,
    lookup_ref,
    query_ref,
    kvq_ref,
    assembled,
    spread,
    keyed,
    pooled,
    weight_t,
    bands,
    *phis,
):
    step = pl.program_id(0)
    steps = pl.num_programs(0)
    packs = (pack0, pack1, pack2, pack3)
    atoms, width = features_ref.shape
    low_half = lax.broadcasted_iota(jnp.int32, (1, LANES), 1) < LANES // 2
    lane = lax.broadcasted_iota(jnp.int32, (1, LANES), 1)
    edges = edge_ref.shape[1]
    window = BLOCK + 2 * HALO
    group_rows = bands.shape[1]
    groups = edges // GROUP
    pairs = GROUP // LANES

    def inputs_of(group):
        part = slice(group * GROUP, (group + 1) * GROUP)
        edge_ref[:, part] = nn(weight_t[...], phis[group][...]).astype(BF16)

    @pl.when(step == 0)
    def _():
        padded = basis[1]
        place_shards(index_ref, packs, 0, padded, assembled)
        weight_t[:, window:] = assembled[...].T.astype(BF16)
        start = round_up(padded, 16)
        for which in range(3):
            place_shards(index_ref, packs, start + which * quarter, quarter, kvq_ref.at[which])
        gain = vector_of(packs, start + 3 * quarter)
        for ref, start in ((before_ref, 0), (features_ref, HALO), (after_ref, HALO + atoms)):
            normed, _ = rms(ref[...].astype(F32))
            lookup_ref[start : start + ref.shape[0], :] = (normed * gain).astype(BF16)
        query = nn(lookup_ref[HALO : HALO + atoms, :], kvq_ref[0]).astype(BF16)
        query_ref[...] = query
        spread_heads(query.astype(F32), spread)
        keyed[...] = (nt(wide(spread).astype(BF16), kvq_ref[1]) * scale).astype(BF16)
        bands[...] = jnp.zeros_like(bands)

    table = lookup_ref[pl.ds(pl.multiple_of(step * BLOCK, BLOCK), window), :]
    weight_t[:, :window] = table.astype(F32).T.astype(BF16)
    geometry = (scaled_ref, heights_ref, relative_ref)
    write_group(geometry, 0, basis, window, phis[0])
    for group in range(groups):
        if group + 1 < groups:
            write_group(geometry, group + 1, basis, window, phis[group + 1])
        inputs_of(group)

    base = pl.multiple_of(step * BLOCK * HEADS, BLOCK * HEADS)
    scores = []
    for tile in range(edges // TILE):
        left = keyed[pl.ds(base + tile * 32, 32), :]
        right = edge_ref[:, tile * TILE : (tile + 1) * TILE]
        for side, score in enumerate(diagonal(nn(left, right), low_half)):
            pair = 2 * tile + side
            low_count = counts_ref[step * BLOCK + pair]
            high_count = counts_ref[step * BLOCK + PAIRS + pair]
            usable = lane < jnp.where(low_half, low_count, high_count + LANES // 2)
            scores.append(jnp.where(usable, score, -1e30))
    score = jnp.concatenate(scores, axis=0)
    power = jnp.exp(score - half_max(score, low_half))
    power_ref[...] = power.astype(BF16)
    ones = jnp.ones((GROUP, LANES), BF16)
    for pair in range(PAIRS):
        group, place = pair // pairs, pair % pairs
        bands[
            group, place * 16 : (place + 1) * 16, place * LANES : (place + 1) * LANES
        ] = block_rows(power[pair * 8 : (pair + 1) * 8], low_half)
    for group in range(groups):
        band = bands[group]
        inverse = 1.0 / nn(band, ones)
        result = nt(band, edge_ref[:, group * GROUP : (group + 1) * GROUP])
        rows = slice(group * group_rows, (group + 1) * group_rows)
        inverse_ref[rows, :] = inverse
        for half in range(width // LANES):
            lanes = slice(half * LANES, (half + 1) * LANES)
            value = result[:, lanes] * inverse
            pooled[half, pl.ds(base + group * group_rows, group_rows), :] = value
            pooled_ref[rows, lanes] = value.astype(BF16)

    @pl.when(step + 1 == steps)
    def _():
        attended_ref[...] = gather_heads(pooled, kvq_ref[2], atoms).astype(BF16)


def forward_call(index, counts, features, before, after, packs, geometry, basis, quarter):
    atoms, width = features.shape
    blocks = atoms // BLOCK
    rows = len(packs) * basis[1]
    slots = LANES // 2
    edges = BLOCK * slots
    table = atoms + 2 * HALO
    full = lambda shape: pl.BlockSpec(shape, lambda b: (0,) * len(shape))
    head_rows = atoms * HEADS
    window = BLOCK + 2 * HALO
    group_rows = GROUP // slots * HEADS
    return pl.pallas_call(
        functools.partial(
            forward_kernel,
            basis,
            quarter,
            (width // HEADS) ** -0.5,
        ),
        grid=(blocks,),
        out_shape=(
            jax.ShapeDtypeStruct((blocks, width, edges), BF16),
            jax.ShapeDtypeStruct((blocks, PAIRS * HEADS, LANES), BF16),
            jax.ShapeDtypeStruct((head_rows, LANES), F32),
            jax.ShapeDtypeStruct((head_rows, width), BF16),
            jax.ShapeDtypeStruct((atoms, width), BF16),
            jax.ShapeDtypeStruct((table, width), BF16),
            jax.ShapeDtypeStruct((atoms, width), BF16),
            jax.ShapeDtypeStruct((3, width, width), BF16),
        ),
        in_specs=[
            pl.BlockSpec(memory_space=pltpu.SMEM),
            pl.BlockSpec(memory_space=pltpu.SMEM),
            full((atoms, width)),
            full((HALO, width)),
            full((HALO, width)),
        ]
        + [full(pack.shape) for pack in packs]
        + [pl.BlockSpec((None, PAIRS, LANES), lambda b: (b, 0, 0))] * 3,
        out_specs=(
            pl.BlockSpec((None, width, edges), lambda b: (b, 0, 0)),
            pl.BlockSpec((None, PAIRS * HEADS, LANES), lambda b: (b, 0, 0)),
            pl.BlockSpec((BLOCK * HEADS, LANES), lambda b: (b, 0)),
            pl.BlockSpec((BLOCK * HEADS, width), lambda b: (b, 0)),
            full((atoms, width)),
            full((table, width)),
            full((atoms, width)),
            full((3, width, width)),
        ),
        scratch_shapes=[
            pltpu.VMEM((rows, width), F32),
            pltpu.VMEM((width // LANES, head_rows, LANES), F32),
            pltpu.VMEM((head_rows, width), BF16),
            pltpu.VMEM((width // LANES, head_rows, LANES), F32),
            pltpu.VMEM((width, window + rows), BF16),
            pltpu.VMEM((edges // GROUP, group_rows, GROUP), BF16),
        ]
        + [pltpu.VMEM((window + rows, GROUP), BF16)] * (edges // GROUP),
        compiler_params=pltpu.CompilerParams(vmem_limit_bytes=24 * 2**20),
        cost_estimate=pl.CostEstimate(
            flops=2 * atoms * slots * width * (rows + window + 64),
            bytes_accessed=2 * atoms * slots * (rows + width),
            transcendentals=atoms * slots * rows,
        ),
        name="attention_forward",
    )(index, counts, features, before, after, *packs, *geometry)


def ffn_kernel(
    quarter,
    small_row,
    index_ref,
    features_ref,
    attended_ref,
    grad_out_ref,
    grad_energy_ref,
    small0,
    small1,
    small2,
    small3,
    pack0,
    pack1,
    pack2,
    pack3,
    out_ref,
    energy_ref,
    grad_residual_ref,
    grad_attended_ref,
    sums_ref,
    grads0,
    grads1,
    grads2,
    grads3,
    w_gate,
    w_up,
    w_down,
    w_out,
    g_gate,
    g_up,
    g_down,
    g_out,
):
    small = (small0, small1, small2, small3)
    packs = (pack0, pack1, pack2, pack3)
    atoms, width = features_ref.shape
    parts = w_gate.shape[1] // width
    down_rows = w_down.shape[0] // 4
    me = index_ref[0]
    for offset, pack in enumerate(packs):
        owner = lax.bitwise_xor(me, offset)
        rows = pl.ds(pl.multiple_of(owner * quarter, 16), quarter)
        for part in range(parts):
            lanes = slice(part * width, (part + 1) * width)
            w_gate[rows, lanes] = pack[part * quarter : (part + 1) * quarter, :]
            w_up[rows, lanes] = pack[(parts + part) * quarter : (parts + part + 1) * quarter, :]
        start = 2 * parts * quarter
        w_down[pl.ds(pl.multiple_of(owner * down_rows, 16), down_rows), :] = pack[
            start : start + down_rows, :
        ]
        w_out[rows, :] = pack[start + down_rows : start + down_rows + quarter, :]
    gain = vector_of(small, small_row + 1)
    readout = vector_of(small, small_row + 2)

    attended = attended_ref[...]
    residual = features_ref[...].astype(F32) + nn(attended, w_out[...])
    normed, inverse = rms(residual)
    hidden = (normed * gain).astype(BF16)
    gate = nn(hidden, w_gate[...])
    up = nn(hidden, w_up[...])
    sigmoid = jax.nn.sigmoid(gate)
    silu = gate * sigmoid
    activated = (silu * up).astype(BF16)
    outputs = residual + nn(activated, w_down[...])
    out_ref[...] = outputs
    energy = jnp.sum(outputs * readout, -1, keepdims=True)
    energy_ref[...] = jnp.broadcast_to(energy, (atoms, LANES)).T[:1, :]
    grad_energy = jnp.broadcast_to(grad_energy_ref[...], (LANES, atoms)).T[:, :1]
    grad_act = grad_out_ref[...].astype(F32) + grad_energy * readout
    grad_branch = grad_act.astype(BF16)
    g_down[...] = tn(activated, grad_branch)
    grad_activated = nt(grad_branch, w_down[...])
    grad_gate = (grad_activated * up * sigmoid * (1.0 + gate * (1.0 - sigmoid))).astype(BF16)
    grad_up = (grad_activated * silu).astype(BF16)
    g_gate[...] = tn(hidden, grad_gate)
    g_up[...] = tn(hidden, grad_up)
    grad_hidden = (nt(grad_gate, w_gate[...]) + nt(grad_up, w_up[...])).astype(BF16).astype(F32)
    grad_residual = grad_act + norm_back(grad_hidden * gain, normed, inverse)
    grad_residual_ref[...] = grad_residual
    grad_proj = grad_residual.astype(BF16)
    grad_attended_ref[...] = nt(grad_proj, w_out[...]).astype(BF16)
    g_out[...] = tn(attended, grad_proj)
    for offset, grads in enumerate((grads0, grads1, grads2, grads3)):
        owner = lax.bitwise_xor(me, offset)
        rows = pl.ds(pl.multiple_of(owner * quarter, 16), quarter)
        row = 0
        for grad in (g_gate, g_up):
            for part in range(parts):
                lanes = slice(part * width, (part + 1) * width)
                grads[row : row + quarter, :] = grad[rows, lanes].astype(BF16)
                row += quarter
        down = pl.ds(pl.multiple_of(owner * down_rows, 16), down_rows)
        grads[row : row + down_rows, :] = g_down[down, :].astype(BF16)
        row += down_rows
        grads[row : row + quarter, :] = g_out[rows, :].astype(BF16)
    sums_ref[...] = jnp.zeros_like(sums_ref)
    sums_ref[1:2, :] = jnp.sum(grad_hidden * normed, 0, keepdims=True)
    sums_ref[2:3, :] = jnp.sum(grad_energy * outputs, 0, keepdims=True)


def ffn_call(index, features, attended, grad_out, grad_energy, small, packs, hidden, quarter, row):
    atoms, width = features.shape
    vmem = pl.BlockSpec(memory_space=pltpu.VMEM)
    return pl.pallas_call(
        functools.partial(ffn_kernel, quarter, row),
        out_shape=(
            jax.ShapeDtypeStruct((atoms, width), F32),
            jax.ShapeDtypeStruct((1, atoms), F32),
            jax.ShapeDtypeStruct((atoms, width), F32),
            jax.ShapeDtypeStruct((atoms, width), BF16),
            jax.ShapeDtypeStruct((8, width), F32),
        )
        + (jax.ShapeDtypeStruct(packs[0].shape, BF16),) * 4,
        in_specs=[pl.BlockSpec(memory_space=pltpu.SMEM)] + [vmem] * 12,
        out_specs=(vmem,) * 9,
        scratch_shapes=[
            pltpu.VMEM(shape, dtype)
            for dtype in (BF16, F32)
            for shape in ((width, hidden), (width, hidden), (hidden, width), (width, width))
        ],
        compiler_params=pltpu.CompilerParams(vmem_limit_bytes=24 * 2**20),
        cost_estimate=pl.CostEstimate(
            flops=18 * atoms * width * hidden, bytes_accessed=2**23, transcendentals=atoms * hidden
        ),
        name="feed_forward",
    )(index, features, attended, grad_out, grad_energy, *small, *packs)


def score_kernel(
    quarter,
    scale,
    index_ref,
    lookup_ref,
    query_ref,
    kvq_ref,
    pooled_ref,
    inverse_ref,
    attended_ref,
    grad_attended_ref,
    power_ref,
    edge_ref,
    grad_score_ref,
    mixed_ref,
    grad_query_ref,
    grads0,
    grads1,
    grads2,
    grads3,
    spread_q,
    spread_g,
    scaled,
    valued,
    means,
    bands,
    pooled,
    weight_grad,
):
    step = pl.program_id(0)
    atoms, width = query_ref.shape
    low_half = lax.broadcasted_iota(jnp.int32, (1, LANES), 1) < LANES // 2
    edges = edge_ref.shape[1]
    group_rows = bands.shape[1]
    groups = edges // GROUP
    pairs = GROUP // LANES

    @pl.when(step == 0)
    def _():
        grad_attended = grad_attended_ref[...].astype(F32)
        product = grad_attended * attended_ref[...].astype(F32)
        high = product.astype(BF16)
        low = (product - high.astype(F32)).astype(BF16)
        heads = lax.broadcasted_iota(jnp.int32, (width, HEADS * LANES), 0) // (width // HEADS)
        copies = lax.broadcasted_iota(jnp.int32, (width, HEADS * LANES), 1) // LANES
        summing = jnp.where(heads == copies, 1.0, 0.0).astype(BF16)
        mean = nn(high, summing) + nn(low, summing)
        for start in range(0, atoms, PAIRS):
            block, side = start // BLOCK, (start % BLOCK) // PAIRS
            for head in range(HEADS):
                place = block * BLOCK * HEADS + side * HEADS + head
                means[pl.ds(place, PAIRS, stride=2 * HEADS), :] = mean[
                    start : start + PAIRS, head * LANES : (head + 1) * LANES
                ]
        inverse = inverse_ref[...]
        means[...] = means[...] * inverse
        spread_heads(query_ref[...].astype(F32), pooled)
        spread_q[...] = wide(pooled).astype(BF16)
        spread_heads(grad_attended, pooled)
        spread_g[...] = wide(pooled).astype(BF16)
        scaled[...] = (wide(pooled) * jnp.concatenate([inverse] * (width // LANES), axis=1)).astype(
            BF16
        )
        valued[...] = nt(scaled[...], kvq_ref[2]).astype(BF16)
        bands[...] = jnp.zeros_like(bands)

    rows = BLOCK * HEADS
    base = pl.multiple_of(step * rows, rows)
    for group in range(groups):
        place = pl.ds(base + group * group_rows, group_rows)
        mixed_ref[group, :, :group_rows] = (nt(kvq_ref[1], spread_q[place, :]) * scale).astype(BF16)
        mixed_ref[group, :, group_rows:] = nt(kvq_ref[2], scaled[place, :]).astype(BF16)
    power = power_ref[...].astype(F32)
    for tile in range(edges // TILE):
        place = pl.ds(base + tile * 32, 32)
        product = nn(valued[place, :], edge_ref[:, tile * TILE : (tile + 1) * TILE])
        for side, grad_soft in enumerate(diagonal(product, low_half, means[place, :])):
            pair = 2 * tile + side
            own = slice(pair * 8, (pair + 1) * 8)
            group, column = pair // pairs, pair % pairs
            value = power[own] * grad_soft
            grad_score_ref[own, :] = value
            bands[
                group, column * 16 : (column + 1) * 16, column * LANES : (column + 1) * LANES
            ] = block_rows(value, low_half)
    for group in range(groups):
        result = nt(bands[group], edge_ref[:, group * GROUP : (group + 1) * GROUP])
        for half in range(width // LANES):
            pooled[half, pl.ds(base + group * group_rows, group_rows), :] = result[
                :, half * LANES : (half + 1) * LANES
            ]

    @pl.when(step == pl.num_programs(0) - 1)
    def _():
        grad_query = (gather_heads(pooled, kvq_ref[1], atoms) * scale).astype(BF16)
        grad_query_ref[...] = grad_query
        weight_grad[0] = tn(lookup_ref[HALO : HALO + atoms, :], grad_query)
        weight_grad[1] = tn(wide(pooled).astype(BF16), spread_q[...]) * scale
        weight_grad[2] = tn(pooled_ref[...], spread_g[...])
        me = index_ref[0]
        for offset, grads in enumerate((grads0, grads1, grads2, grads3)):
            owner = lax.bitwise_xor(me, offset)
            rows = pl.ds(pl.multiple_of(owner * quarter, 16), quarter)
            for which in range(3):
                grads[which * quarter : (which + 1) * quarter, :] = weight_grad[
                    which, rows, :
                ].astype(BF16)


def score_call(
    index, lookup, query, kvq, pooled, inverse, attended, grad_attended, power, edge, quarter
):
    atoms, width = query.shape
    blocks, _, edges = edge.shape
    head_rows = atoms * HEADS
    group_rows = GROUP // (edges // BLOCK) * HEADS
    groups = edges // GROUP
    full = lambda shape: pl.BlockSpec(shape, lambda b: (0,) * len(shape))
    whole = (lookup, query, kvq, pooled, inverse, attended, grad_attended)
    pair_block = pl.BlockSpec((None, PAIRS * HEADS, LANES), lambda b: (b, 0, 0))
    grads = (3 * quarter, width)
    return pl.pallas_call(
        functools.partial(score_kernel, quarter, (width // HEADS) ** -0.5),
        grid=(blocks,),
        out_shape=(
            jax.ShapeDtypeStruct((blocks, PAIRS * HEADS, LANES), F32),
            jax.ShapeDtypeStruct((blocks * groups, width, 2 * group_rows), BF16),
            jax.ShapeDtypeStruct((atoms, width), BF16),
        )
        + (jax.ShapeDtypeStruct(grads, BF16),) * 4,
        in_specs=[pl.BlockSpec(memory_space=pltpu.SMEM)]
        + [full(value.shape) for value in whole]
        + [pair_block, pl.BlockSpec((None, width, edges), lambda b: (b, 0, 0))],
        out_specs=(
            pair_block,
            pl.BlockSpec((groups, width, 2 * group_rows), lambda b: (b, 0, 0)),
            full((atoms, width)),
        )
        + (full(grads),) * 4,
        scratch_shapes=[
            pltpu.VMEM((head_rows, width), BF16),
            pltpu.VMEM((head_rows, width), BF16),
            pltpu.VMEM((head_rows, width), BF16),
            pltpu.VMEM((head_rows, width), BF16),
            pltpu.VMEM((head_rows, LANES), F32),
            pltpu.VMEM((groups, group_rows, GROUP), BF16),
            pltpu.VMEM((width // LANES, head_rows, LANES), F32),
            pltpu.VMEM((3, width, width), F32),
        ],
        compiler_params=pltpu.CompilerParams(vmem_limit_bytes=24 * 2**20),
        cost_estimate=pl.CostEstimate(
            flops=2 * atoms * edges // BLOCK * width * 256,
            bytes_accessed=2 * blocks * width * edges,
            transcendentals=0,
        ),
        name="score_backward",
    )(index, *whole, power, edge)


def edge_kernel(basis, gain_row, first_block, last_block, carried, final, *refs):
    refs = list(refs)
    take = lambda count: [refs.pop(0) for _ in range(count)]
    geometry, (power_ref, grad_score_ref, mixed_ref) = take(3), take(3)
    before = take(2 if carried else 0)
    if final:
        index_ref, features_ref, before_ref, after_ref, grad_query_ref, kvq_ref = take(6)
        grad_residual_ref, sums_ref = take(2)
        small = take(4)
        grad_own_ref, grad_lower_ref, grad_upper_ref = take(3)
        grads_refs = take(4)
    grad_rbf, grad_lookup = take(2)
    (bands,), grad_edges = take(1), take(len(refs) // 2)
    phis = refs
    block = pl.program_id(0) + first_block
    width = mixed_ref.shape[1]
    padded = basis[1]
    window = BLOCK + 2 * HALO
    low_half = lax.broadcasted_iota(jnp.int32, (1, LANES), 1) < LANES // 2
    group_rows = bands.shape[1] // 2
    groups = len(phis)
    pairs = GROUP // LANES

    @pl.when(block == first_block)
    def _():
        bands[...] = jnp.zeros_like(bands)
        if carried:
            grad_rbf[...] = before[0][...]
            grad_lookup[...] = before[1][...]
        else:
            grad_rbf[...] = jnp.zeros_like(grad_rbf)
            grad_lookup[...] = jnp.zeros_like(grad_lookup)

    power = power_ref[...].astype(F32)
    grad_score = grad_score_ref[...]
    for pair in range(PAIRS):
        group, column = pair // pairs, pair % pairs
        own = slice(pair * 8, (pair + 1) * 8)
        lanes = slice(column * LANES, (column + 1) * LANES)
        for start, value in ((0, grad_score[own]), (group_rows, power[own])):
            row = start + column * 16
            bands[group, row : row + 16, lanes] = block_rows(value, low_half)
    for group in range(groups):
        grad_edges[group][...] = nn(mixed_ref[group], bands[group]).astype(BF16)
    write_group(geometry, 0, basis, window, phis[0])
    total = None
    for group in range(groups):
        if group + 1 < groups:
            write_group(geometry, group + 1, basis, window, phis[group + 1])
        term = nt(phis[group][...], grad_edges[group][...])
        total = term if total is None else total + term
    grad_lookup[pl.ds(pl.multiple_of(block * BLOCK, BLOCK), window), :] += total[:window]
    grad_rbf[...] += total[window:]

    if not final:
        return

    @pl.when(block == last_block - 1)
    def _():
        atoms = features_ref.shape[0]
        grad_lookup[HALO : HALO + atoms, :] += nt(grad_query_ref[...], kvq_ref[0])
        gain = vector_of(small, gain_row)
        grad_gain = jnp.zeros((1, width), F32)
        places = (
            (before_ref, 0, grad_lower_ref),
            (features_ref, HALO, grad_own_ref),
            (after_ref, HALO + atoms, grad_upper_ref),
        )
        for ref, start, out in places:
            normed, inverse = rms(ref[...].astype(F32))
            grad = grad_lookup[start : start + ref.shape[0], :]
            grad_gain = grad_gain + jnp.sum(grad * normed, 0, keepdims=True)
            back = norm_back(grad * gain, normed, inverse)
            if start == HALO:
                back = back + grad_residual_ref[...]
            out[...] = back.astype(out.dtype)
        vectors = jnp.concatenate([grad_gain, sums_ref[1:8, :], jnp.zeros((8, width), F32)], 0)
        after_rbf = round_up(padded, 16)
        rest = jnp.zeros((after_rbf - padded, width), F32)
        me = index_ref[0]
        for offset, grads in enumerate(grads_refs):
            owner = lax.bitwise_xor(me, offset)
            rbf = grad_rbf[pl.ds(pl.multiple_of(owner * padded, 8), padded), :]
            grads[:after_rbf, :] = jnp.concatenate([rbf, rest], 0).astype(BF16)
            grads[after_rbf:, :] = vectors.astype(BF16)


def edge_call(arrays, carry, last, basis, members, gain_row, first_block, last_block):
    width = arrays[-1].shape[1]
    blocks = arrays[0].shape[0]
    rows, edges = members * basis[1], PAIRS * LANES
    groups = edges // GROUP
    group_rows = GROUP // (edges // BLOCK) * HEADS
    table = blocks * BLOCK + 2 * HALO
    window = BLOCK + 2 * HALO
    full = lambda shape: pl.BlockSpec(shape, lambda b: (0,) * len(shape))
    here = lambda b: (b + first_block, 0, 0)
    in_specs = [
        pl.BlockSpec((None, PAIRS, LANES), here),
        pl.BlockSpec((None, PAIRS, LANES), here),
        pl.BlockSpec((None, PAIRS, LANES), here),
        pl.BlockSpec((None, PAIRS * HEADS, LANES), here),
        pl.BlockSpec((None, PAIRS * HEADS, LANES), here),
        pl.BlockSpec((groups, width, 2 * group_rows), here),
    ]
    operands = list(arrays)
    sums = [(rows, width), (table, width)]
    if carry is not None:
        in_specs += [full(value.shape) for value in carry]
        operands += list(carry)
    scratch = [pltpu.VMEM((groups, 2 * group_rows, GROUP), BF16)]
    scratch += [pltpu.VMEM((width, GROUP), BF16)] * groups
    scratch += [pltpu.VMEM((window + rows, GROUP), BF16)] * groups
    if last is None:
        shapes = [(shape, F32) for shape in sums]
    else:
        in_specs += [pl.BlockSpec(memory_space=pltpu.SMEM)]
        in_specs += [full(value.shape) for value in last[1:]]
        operands += list(last)
        grads = (round_up(basis[1], 16) + 16, width)
        shapes = [((blocks * BLOCK, width), F32)] + [((HALO, width), BF16)] * 2 + [(grads, BF16)] * 4
        scratch = [pltpu.VMEM(shape, F32) for shape in sums] + scratch
    return pl.pallas_call(
        functools.partial(
            edge_kernel, basis, gain_row, first_block, last_block, carry is not None, last is not None
        ),
        grid=(last_block - first_block,),
        out_shape=[jax.ShapeDtypeStruct(shape, dtype) for shape, dtype in shapes],
        in_specs=in_specs,
        out_specs=[full(shape) for shape, _ in shapes],
        scratch_shapes=scratch,
        compiler_params=pltpu.CompilerParams(vmem_limit_bytes=24 * 2**20),
        cost_estimate=pl.CostEstimate(
            flops=2 * (last_block - first_block) * edges * width * (rows + window + 256),
            bytes_accessed=2**22,
            transcendentals=(last_block - first_block) * rows * edges,
        ),
        name="edge_backward",
    )(*operands)


def large_kernel(first, second, gate, up, down, out):
    total = lambda rows: first[rows, :].astype(F32) + second[rows, :].astype(F32)
    quarter, width = out.shape
    row = 0
    for ref in (gate, up):
        for part in range(ref.shape[1] // width):
            ref[:, part * width : (part + 1) * width] = total(slice(row, row + quarter))
            row += quarter
    for ref in (down, out):
        ref[...] = total(slice(row, row + ref.shape[0]))
        row += ref.shape[0]


def large_call(first, second, quarter, hidden, down_rows):
    width = first.shape[1]
    vmem = pl.BlockSpec(memory_space=pltpu.VMEM)
    shapes = ((quarter, hidden), (quarter, hidden), (down_rows, width), (quarter, width))
    return pl.pallas_call(
        large_kernel,
        out_shape=[jax.ShapeDtypeStruct(shape, F32) for shape in shapes],
        in_specs=[vmem] * 2,
        out_specs=[vmem] * 4,
        name="feed_forward_results",
    )(first, second)


def small_kernel(
    index_ref,
    score_first,
    score_second,
    edge_first,
    edge_second,
    grad_own,
    from_lower,
    from_upper,
    rbf,
    query,
    key,
    value,
    gain_attn,
    gain_ffn,
    readout,
    features,
):
    quarter = query.shape[0]
    width = query.shape[1]
    for which, ref in enumerate((query, key, value)):
        rows = slice(which * quarter, (which + 1) * quarter)
        ref[...] = score_first[rows, :].astype(F32) + score_second[rows, :].astype(F32)
    total = edge_first[...].astype(F32) + edge_second[...].astype(F32)
    rbf[...] = total[: rbf.shape[0]]
    start = edge_first.shape[0] - 16
    me = index_ref[0]
    for which, ref in enumerate((gain_attn, gain_ffn, readout)):
        row = total[start + which : start + which + 1]
        picked = jnp.zeros((1, quarter), F32)
        for owner in range(width // quarter):
            piece = row[:, owner * quarter : (owner + 1) * quarter]
            picked = picked + jnp.where(me == owner, piece, 0.0)
        ref[...] = picked
    features[...] = grad_own[...]
    features[:HALO, :] += from_lower[...].astype(F32)
    features[features.shape[0] - HALO :, :] += from_upper[...].astype(F32)


def small_call(index, score, edge, grad_own, from_lower, from_upper, shard, quarter):
    width = grad_own.shape[1]
    vmem = pl.BlockSpec(memory_space=pltpu.VMEM)
    shapes = [(shard, width)] + [(quarter, width)] * 3 + [(1, quarter)] * 3 + [grad_own.shape]
    return pl.pallas_call(
        small_kernel,
        out_shape=[jax.ShapeDtypeStruct(shape, F32) for shape in shapes],
        in_specs=[pl.BlockSpec(memory_space=pltpu.SMEM)] + [vmem] * 7,
        out_specs=[vmem] * 8,
        name="edge_results",
    )(index, *score, *edge, grad_own, from_lower, from_upper)


def exchange(value, axis, offset):
    size = lax.axis_size(axis)
    return lax.ppermute(value, axis, [(i, i ^ offset) for i in range(size)])


def shifted(value, by):
    axes = ("space", "wt")
    size = lax.axis_size(axes)
    pairs = [(i, i + by) for i in range(size) if 0 <= i + by < size]
    return lax.ppermute(value, axes, pairs)


def gathered(value):
    return [value] + [exchange(value, "wt", offset) for offset in range(1, lax.axis_size("wt"))]


def added(*values):
    total = values[0].astype(F32)
    for value in values[1:]:
        total = total + value.astype(F32)
    return total.astype(values[0].dtype)


class Reduction:
    def __init__(self, chunks):
        self.offsets = [1 << bit for bit in range(lax.axis_size("space").bit_length() - 1)]
        self.terms = [chunks[0]] + [
            exchange(chunk, "wt", offset) for offset, chunk in enumerate(chunks[1:], 1)
        ]

    def add(self):
        if self.offsets:
            self.terms = [added(*self.terms)]

    def send(self):
        if self.offsets:
            self.terms.append(exchange(self.terms[0], "space", self.offsets.pop(0)))

    def finish(self):
        while self.offsets:
            self.add()
            self.send()
        return self.terms


def between(reductions, value):
    terms = [reduction.terms for reduction in reductions]
    terms, value = lax.optimization_barrier((terms, value))
    for reduction, own in zip(reductions, terms):
        reduction.terms = list(own)
        reduction.add()
    terms = [reduction.terms for reduction in reductions]
    terms, value = lax.optimization_barrier((terms, value))
    for reduction, own in zip(reductions, terms):
        reduction.terms = list(own)
        reduction.send()
    return value


SPLIT = (2, 2, 2)


def local(
    features,
    distances,
    neighbours,
    counts,
    rbf_weight,
    query_weight,
    key_weight,
    value_weight,
    out_weight,
    gate_weight,
    up_weight,
    down_weight,
    attn_gain,
    ffn_gain,
    readout,
    grad_out,
    grad_energy,
):
    members = lax.axis_size("wt")
    atoms, width = features.shape
    shard = rbf_weight.shape[0]
    padded = round_up(shard, 8)
    factor = basis_factor(members * shard)
    basis = (shard, padded, factor * CUTOFF / (members * shard))
    gain_row = round_up(shard, 16) + 3 * query_weight.shape[0]
    quarter = query_weight.shape[0]
    hidden = gate_weight.shape[1]
    index = lax.axis_index("wt").astype(jnp.int32)[None]

    small, large, initial, final = pack_call(
        index,
        rbf_weight,
        query_weight,
        key_weight,
        value_weight,
        out_weight,
        gate_weight,
        up_weight,
        down_weight,
        attn_gain[None],
        ffn_gain[None],
        readout[None],
        features,
    )
    small_all = gathered(small)
    before = shifted(final, 1)
    after = shifted(initial, -1)
    geometry = geometry_call(distances.T, neighbours.T, factor)
    large, geometry = lax.optimization_barrier((large, geometry))
    large_all = gathered(large)

    edge, power, inverse, pooled, attended, lookup, query, kvq = forward_call(
        index, counts, features, before, after, small_all, geometry, basis, quarter
    )
    outputs, energy, grad_residual, grad_attended, sums, *large_grads = ffn_call(
        index,
        features,
        attended,
        grad_out,
        grad_energy[None, :],
        small_all,
        large_all,
        hidden,
        quarter,
        gain_row,
    )
    grad_score, mixed, grad_query, *score_grads = score_call(
        index, lookup, query, kvq, pooled, inverse, attended, grad_attended, power, edge, quarter
    )
    large_sum, score_sum = Reduction(large_grads), Reduction(score_grads)
    carry, block = None, 0
    last = (index, features, before, after, grad_query, kvq, grad_residual, sums, *small_all)
    for count in SPLIT:
        if carry is None:
            grad_score = between([large_sum], grad_score)
        else:
            carry = between([large_sum, score_sum], carry)
        final = block + count == edge.shape[0]
        carry = edge_call(
            (*geometry, power, grad_score, mixed),
            carry,
            last if final else None,
            basis,
            members,
            gain_row,
            block,
            block + count,
        )
        block += count
    grad_own, grad_lower, grad_upper, *edge_grads = carry
    edge_sum = Reduction(edge_grads)
    from_upper = shifted(grad_lower, -1)
    from_lower = shifted(grad_upper, 1)
    score_sum = score_sum.finish()
    results = large_call(*large_sum.finish(), quarter, hidden, down_weight.shape[0])
    grad_gate, grad_up, grad_down, grad_out_w = between([edge_sum], results)
    edge_sum = edge_sum.finish()
    grad_rbf, grad_q, grad_k, grad_v, grad_attn, grad_ffn, grad_read, grad_features = small_call(
        index, score_sum, edge_sum, grad_own, from_lower, from_upper, shard, quarter
    )
    return (
        outputs,
        energy[0],
        grad_features,
        grad_rbf,
        grad_q,
        grad_k,
        grad_v,
        grad_out_w,
        grad_gate,
        grad_up,
        grad_down,
        grad_attn[0],
        grad_ffn[0],
        grad_read[0],
    )


def solution(mesh):
    rows = P(("space", "wt"), None)
    line = P(("space", "wt"))
    in_specs = (rows, rows, rows, line) + (P("wt", None),) * 8 + (P("wt"),) * 3 + (rows, line)
    out_specs = (rows, line, rows) + (P("wt", None),) * 8 + (P("wt"),) * 3
    return jax.shard_map(local, mesh=mesh, in_specs=in_specs, out_specs=out_specs, check_vma=False)
```

```python
import functools
import math

import jax
import jax.numpy as jnp
from jax import lax
from jax.experimental import pallas as pl
from jax.experimental.pallas import tpu as pltpu
from jax.sharding import PartitionSpec as P

HEADS = 8
HALO = 96
EPSILON = 1e-06
CUTOFF = 6.0

BLOCK = 64
PAIRS = BLOCK // 2
LANES = 128
TILE = 256
GROUP = 1024

BF16 = jnp.bfloat16
F32 = jnp.float32


def nn(a, b):
    return lax.dot_general(a, b, (((1,), (0,)), ((), ())), preferred_element_type=F32)


def nt(a, b):
    return lax.dot_general(a, b, (((1,), (1,)), ((), ())), preferred_element_type=F32)


def tn(a, b):
    return lax.dot_general(a, b, (((0,), (0,)), ((), ())), preferred_element_type=F32)


def round_up(value, step):
    return -(-value // step) * step


def rms(value):
    inverse = lax.rsqrt(jnp.mean(value * value, -1, keepdims=True) + EPSILON)
    return value * inverse, inverse


def norm_back(grad_normed, normed_rows, inverse):
    return inverse * (
        grad_normed - normed_rows * jnp.mean(grad_normed * normed_rows, -1, keepdims=True)
    )


def pair_rows(block):
    return jnp.concatenate([block[:PAIRS], block[PAIRS:]], axis=1)


def head_of_lane(width):
    return lax.broadcasted_iota(jnp.int32, (1, width), 1) // (width // HEADS)


def spread_heads(rows, out_ref):
    atoms, width = rows.shape
    heads = head_of_lane(width)
    for start in range(0, atoms, PAIRS):
        block, side = start // BLOCK, (start % BLOCK) // PAIRS
        part = rows[start : start + PAIRS]
        for head in range(HEADS):
            place = block * BLOCK * HEADS + side * HEADS + head
            kept = jnp.where(heads == head, part, 0.0)
            for half in range(width // LANES):
                out_ref[half, pl.ds(place, PAIRS, stride=2 * HEADS), :] = kept[
                    :, half * LANES : (half + 1) * LANES
                ]


def wide(ref, rows=slice(None)):
    return jnp.concatenate([ref[half, rows, :] for half in range(ref.shape[0])], axis=1)


def gather_heads(rows_ref, weight, atoms):
    heads = head_of_lane(weight.shape[1])
    lefts, rights = [], []
    for head in range(HEADS):
        parts = []
        for start in range(0, atoms, PAIRS):
            block, side = start // BLOCK, (start % BLOCK) // PAIRS
            place = block * BLOCK * HEADS + side * HEADS + head
            parts.append(wide(rows_ref, pl.ds(place, PAIRS, stride=2 * HEADS)))
        lefts.append(jnp.concatenate(parts, axis=0).astype(BF16))
        rights.append(jnp.where(heads == head, weight, jnp.zeros_like(weight)))
    return nn(jnp.concatenate(lefts, axis=1), jnp.concatenate(rights, axis=0))


def half_max(value, low_half):
    low = jnp.max(jnp.where(low_half, value, -jnp.inf), axis=1, keepdims=True)
    high = jnp.max(jnp.where(low_half, -jnp.inf, value), axis=1, keepdims=True)
    return jnp.where(low_half, low, high)


def write_onehot(relative, window, out_ref):
    relative = relative.astype(BF16)
    one, zero = jnp.ones((), BF16), jnp.zeros((), BF16)
    place = lax.broadcasted_iota(jnp.int32, (16, LANES), 0).astype(F32)
    pairs = range(relative.shape[0])
    wanted = [jnp.broadcast_to(relative[pair : pair + 1, :], (16, LANES)) for pair in pairs]
    for row in range(0, window, 16):
        here = (place + float(row)).astype(BF16)
        for pair in pairs:
            out_ref[row : row + 16, pair * LANES : (pair + 1) * LANES] = jnp.where(
                here == wanted[pair], one, zero
            )


def write_basis(scaled, heights, shard, padded, step, window, out_ref):
    iota = lax.broadcasted_iota(jnp.int32, (8, LANES), 0).astype(F32) * step
    center = lambda row: ((row // padded) * shard + row % padded) * step
    pairs = range(scaled.shape[0])
    bases = [scaled[pair : pair + 1, :] - iota for pair in pairs]
    tops = [
        jnp.broadcast_to(heights[pair : pair + 1, :], (16, LANES)).astype(BF16) for pair in pairs
    ]
    for row in range(0, out_ref.shape[0] - window, 16):
        for pair, base, top in zip(pairs, bases, tops):
            delta = jnp.concatenate([base - center(row), base - center(row + 8)], axis=0)
            low = delta.astype(BF16)
            value = jnp.exp2(-(low * low)) * top
            out_ref[window + row : window + row + 16, pair * LANES : (pair + 1) * LANES] = value


def write_group(geometry, group, basis, window, out_ref):
    pairs = GROUP // LANES
    scaled, heights, relative = (
        geometry[which, group * pairs : (group + 1) * pairs, :] for which in range(3)
    )
    write_onehot(relative, window, out_ref)
    write_basis(scaled, heights, *basis, window, out_ref)


def diagonal(tile, low_half, less=None):
    parts = []
    for side in range(2):
        lanes = slice(side * LANES, (side + 1) * LANES)
        rows = [slice(side * 16 + part * 8, side * 16 + part * 8 + 8) for part in range(2)]
        both = [tile[row, lanes] if less is None else tile[row, lanes] - less[row] for row in rows]
        parts.append(jnp.where(low_half, both[0], both[1]))
    return parts


def block_rows(value, low_half):
    zero = jnp.zeros_like(value)
    return jnp.concatenate(
        [jnp.where(low_half, value, zero), jnp.where(low_half, zero, value)], axis=0
    ).astype(BF16)


def pack_kernel(
    index_ref,
    rbf_ref,
    query_ref,
    key_ref,
    value_ref,
    out_ref,
    gate_ref,
    up_ref,
    down_ref,
    attn_ref,
    ffn_ref,
    read_ref,
    features_ref,
    small_ref,
    large_ref,
    initial_ref,
    final_ref,
):
    initial_ref[...] = features_ref[:HALO, :]
    final_ref[...] = features_ref[features_ref.shape[0] - HALO :, :]
    shard, width = rbf_ref.shape
    quarter = query_ref.shape[0]
    after_rbf = round_up(shard, 16)
    rest = jnp.zeros((after_rbf - shard, width), F32)
    small_ref[:after_rbf, :] = jnp.concatenate([rbf_ref[...].astype(F32), rest], 0).astype(BF16)
    row = after_rbf
    for ref in (query_ref, key_ref, value_ref):
        small_ref[row : row + quarter, :] = ref[...]
        row += quarter
    vectors = jnp.concatenate([ref[...].astype(F32) for ref in (attn_ref, ffn_ref, read_ref)], 0)
    copies = jnp.concatenate([vectors] * (width // quarter), axis=1)
    owner = lax.broadcasted_iota(jnp.int32, (1, width), 1) // quarter
    own = jnp.where(owner == index_ref[0], copies, 0.0)
    small_ref[row : row + 16, :] = jnp.concatenate(
        [own, jnp.zeros((16 - own.shape[0], width), F32)], 0
    ).astype(BF16)
    row = 0
    for ref in (gate_ref, up_ref):
        for part in range(ref.shape[1] // width):
            large_ref[row : row + quarter, :] = ref[:, part * width : (part + 1) * width]
            row += quarter
    for ref in (down_ref, out_ref):
        large_ref[row : row + ref.shape[0], :] = ref[...]
        row += ref.shape[0]


def pack_call(index, rbf, query, key, value, out, gate, up, down, *rest):
    width = rbf.shape[1]
    quarter = query.shape[0]
    vmem = pl.BlockSpec(memory_space=pltpu.VMEM)
    small = round_up(rbf.shape[0], 16) + 3 * quarter + 16
    large = 2 * quarter * (gate.shape[1] // width) + down.shape[0] + quarter
    return pl.pallas_call(
        pack_kernel,
        out_shape=(
            jax.ShapeDtypeStruct((small, width), BF16),
            jax.ShapeDtypeStruct((large, width), BF16),
            jax.ShapeDtypeStruct((HALO, width), BF16),
            jax.ShapeDtypeStruct((HALO, width), BF16),
        ),
        in_specs=[pl.BlockSpec(memory_space=pltpu.SMEM)] + [vmem] * 12,
        out_specs=(vmem,) * 4,
        cost_estimate=pl.CostEstimate(flops=0, bytes_accessed=2**21, transcendentals=0),
        name="pack_weights",
    )(index, rbf, query, key, value, out, gate, up, down, *rest)


def geometry_kernel(factor, dist_ref, rows_ref, out_ref, done_ref):
    dist = dist_ref[...].T
    rows = rows_ref[...].astype(F32).T
    for block in range(out_ref.shape[0]):
        place = slice(block * BLOCK, (block + 1) * BLOCK)
        pairs = pair_rows(dist[place])
        out_ref[block, 0] = pairs * factor
        out_ref[block, 1] = 0.5 * (jnp.cos(jnp.pi * pairs / CUTOFF) + 1.0)
        out_ref[block, 2] = pair_rows(rows[place]) - float(block * BLOCK)
    done_ref[...] = jnp.zeros_like(done_ref)


def geometry_call(distances, neighbours, factor):
    slots, atoms = distances.shape
    blocks = atoms // BLOCK
    vmem = pl.BlockSpec(memory_space=pltpu.VMEM)
    return pl.pallas_call(
        functools.partial(geometry_kernel, factor),
        out_shape=(
            jax.ShapeDtypeStruct((blocks, 3, PAIRS, LANES), F32),
            jax.ShapeDtypeStruct((8, LANES), F32),
        ),
        in_specs=[vmem, vmem],
        out_specs=(vmem,) * 2,
        cost_estimate=pl.CostEstimate(
            flops=40 * atoms * slots, bytes_accessed=20 * atoms * slots, transcendentals=0
        ),
        name="edge_geometry",
    )(distances, neighbours)


def basis_factor(basis_count):
    return math.sqrt(0.5 / math.log(2.0)) * basis_count / (2.0 * CUTOFF)


def place_shards(index_ref, packs, row, count, out_ref):
    me = index_ref[0]
    for offset, pack in enumerate(packs):
        owner = lax.bitwise_xor(me, offset)
        start = pl.multiple_of(owner * count, 8)
        out_ref[pl.ds(start, count), :] = pack[row : row + count, :].astype(out_ref.dtype)


def vector_of(packs, row):
    total = packs[0][row : row + 1, :].astype(F32)
    for pack in packs[1:]:
        total = total + pack[row : row + 1, :].astype(F32)
    return total


def forward_kernel(
    basis,
    quarter,
    scale,
    index_ref,
    counts_ref,
    features_ref,
    before_ref,
    after_ref,
    pack0,
    pack1,
    pack2,
    pack3,
    geometry,
    edge_ref,
    power_ref,
    inverse_ref,
    pooled_ref,
    attended_ref,
    lookup_ref,
    query_ref,
    kvq_ref,
    assembled,
    spread,
    keyed,
    pooled,
    weight_t,
    bands,
    *phis,
):
    step = pl.program_id(0)
    steps = pl.num_programs(0)
    packs = (pack0, pack1, pack2, pack3)
    atoms, width = features_ref.shape
    low_half = lax.broadcasted_iota(jnp.int32, (1, LANES), 1) < LANES // 2
    lane = lax.broadcasted_iota(jnp.int32, (1, LANES), 1)
    edges = edge_ref.shape[1]
    window = BLOCK + 2 * HALO
    group_rows = bands.shape[1]
    groups = edges // GROUP
    pairs = GROUP // LANES

    def inputs_of(group):
        part = slice(group * GROUP, (group + 1) * GROUP)
        edge_ref[:, part] = nn(weight_t[...], phis[group][...]).astype(BF16)

    @pl.when(step == 0)
    def _():
        padded = basis[1]
        place_shards(index_ref, packs, 0, padded, assembled)
        weight_t[:, window:] = assembled[...].T.astype(BF16)
        start = round_up(padded, 16)
        for which in range(3):
            place_shards(index_ref, packs, start + which * quarter, quarter, kvq_ref.at[which])
        gain = vector_of(packs, start + 3 * quarter)
        for ref, start in ((before_ref, 0), (features_ref, HALO), (after_ref, HALO + atoms)):
            normed, _ = rms(ref[...].astype(F32))
            lookup_ref[start : start + ref.shape[0], :] = (normed * gain).astype(BF16)
        query = nn(lookup_ref[HALO : HALO + atoms, :], kvq_ref[0]).astype(BF16)
        query_ref[...] = query
        spread_heads(query.astype(F32), spread)
        keyed[...] = (nt(wide(spread).astype(BF16), kvq_ref[1]) * scale).astype(BF16)
        bands[...] = jnp.zeros_like(bands)

    table = lookup_ref[pl.ds(pl.multiple_of(step * BLOCK, BLOCK), window), :]
    weight_t[:, :window] = table.astype(F32).T.astype(BF16)
    write_group(geometry, 0, basis, window, phis[0])
    for group in range(groups):
        if group + 1 < groups:
            write_group(geometry, group + 1, basis, window, phis[group + 1])
        inputs_of(group)

    base = pl.multiple_of(step * BLOCK * HEADS, BLOCK * HEADS)
    scores = []
    for tile in range(edges // TILE):
        left = keyed[pl.ds(base + tile * 32, 32), :]
        right = edge_ref[:, tile * TILE : (tile + 1) * TILE]
        for side, score in enumerate(diagonal(nn(left, right), low_half)):
            pair = 2 * tile + side
            low_count = counts_ref[step * BLOCK + pair]
            high_count = counts_ref[step * BLOCK + PAIRS + pair]
            usable = lane < jnp.where(low_half, low_count, high_count + LANES // 2)
            scores.append(jnp.where(usable, score, -1e30))
    score = jnp.concatenate(scores, axis=0)
    power = jnp.exp(score - half_max(score, low_half))
    power_ref[...] = power.astype(BF16)
    ones = jnp.ones((GROUP, LANES), BF16)
    for pair in range(PAIRS):
        group, place = pair // pairs, pair % pairs
        bands[
            group, place * 16 : (place + 1) * 16, place * LANES : (place + 1) * LANES
        ] = block_rows(power[pair * 8 : (pair + 1) * 8], low_half)
    for group in range(groups):
        band = bands[group]
        inverse = 1.0 / nn(band, ones)
        result = nt(band, edge_ref[:, group * GROUP : (group + 1) * GROUP])
        rows = slice(group * group_rows, (group + 1) * group_rows)
        inverse_ref[rows, :] = inverse
        for half in range(width // LANES):
            lanes = slice(half * LANES, (half + 1) * LANES)
            value = result[:, lanes] * inverse
            pooled[half, pl.ds(base + group * group_rows, group_rows), :] = value
            pooled_ref[rows, lanes] = value.astype(BF16)

    @pl.when(step + 1 == steps)
    def _():
        attended_ref[...] = gather_heads(pooled, kvq_ref[2], atoms).astype(BF16)


def forward_call(index, counts, features, before, after, packs, geometry, basis, quarter):
    atoms, width = features.shape
    blocks = atoms // BLOCK
    rows = len(packs) * basis[1]
    slots = LANES // 2
    edges = BLOCK * slots
    table = atoms + 2 * HALO
    full = lambda shape: pl.BlockSpec(shape, lambda b: (0,) * len(shape))
    head_rows = atoms * HEADS
    window = BLOCK + 2 * HALO
    group_rows = GROUP // slots * HEADS
    return pl.pallas_call(
        functools.partial(
            forward_kernel,
            basis,
            quarter,
            (width // HEADS) ** -0.5,
        ),
        grid=(blocks,),
        out_shape=(
            jax.ShapeDtypeStruct((blocks, width, edges), BF16),
            jax.ShapeDtypeStruct((blocks, PAIRS * HEADS, LANES), BF16),
            jax.ShapeDtypeStruct((head_rows, LANES), F32),
            jax.ShapeDtypeStruct((head_rows, width), BF16),
            jax.ShapeDtypeStruct((atoms, width), BF16),
            jax.ShapeDtypeStruct((table, width), BF16),
            jax.ShapeDtypeStruct((atoms, width), BF16),
            jax.ShapeDtypeStruct((3, width, width), BF16),
        ),
        in_specs=[
            pl.BlockSpec(memory_space=pltpu.SMEM),
            pl.BlockSpec(memory_space=pltpu.SMEM),
            full((atoms, width)),
            full((HALO, width)),
            full((HALO, width)),
        ]
        + [full(pack.shape) for pack in packs]
        + [pl.BlockSpec((None, 3, PAIRS, LANES), lambda b: (b, 0, 0, 0))],
        out_specs=(
            pl.BlockSpec((None, width, edges), lambda b: (b, 0, 0)),
            pl.BlockSpec((None, PAIRS * HEADS, LANES), lambda b: (b, 0, 0)),
            pl.BlockSpec((BLOCK * HEADS, LANES), lambda b: (b, 0)),
            pl.BlockSpec((BLOCK * HEADS, width), lambda b: (b, 0)),
            full((atoms, width)),
            full((table, width)),
            full((atoms, width)),
            full((3, width, width)),
        ),
        scratch_shapes=[
            pltpu.VMEM((rows, width), F32),
            pltpu.VMEM((width // LANES, head_rows, LANES), F32),
            pltpu.VMEM((head_rows, width), BF16),
            pltpu.VMEM((width // LANES, head_rows, LANES), F32),
            pltpu.VMEM((width, window + rows), BF16),
            pltpu.VMEM((edges // GROUP, group_rows, GROUP), BF16),
        ]
        + [pltpu.VMEM((window + rows, GROUP), BF16)] * (edges // GROUP),
        compiler_params=pltpu.CompilerParams(vmem_limit_bytes=24 * 2**20),
        cost_estimate=pl.CostEstimate(
            flops=2 * atoms * slots * width * (rows + window + 64),
            bytes_accessed=2 * atoms * slots * (rows + width),
            transcendentals=atoms * slots * rows,
        ),
        name="attention_forward",
    )(index, counts, features, before, after, *packs, geometry)


def ffn_kernel(
    quarter,
    small_row,
    index_ref,
    side_ref,
    features_ref,
    attended_ref,
    grad_out_ref,
    grad_energy_ref,
    small0,
    small1,
    small2,
    small3,
    pack0,
    pack1,
    pack2,
    pack3,
    out_ref,
    energy_ref,
    grad_residual_ref,
    grad_attended_ref,
    sums_ref,
    grads0,
    grads1,
    grads2,
    grads3,
    w_gate,
    w_up,
    w_down,
    w_out,
    g_gate,
    g_up,
    g_down,
    g_out,
):
    small = (small0, small1, small2, small3)
    packs = (pack0, pack1, pack2, pack3)
    atoms, width = features_ref.shape
    parts = w_gate.shape[1] // width
    down_rows = w_down.shape[0] // 4
    me = index_ref[0]
    for offset, pack in enumerate(packs):
        owner = lax.bitwise_xor(me, offset)
        rows = pl.ds(pl.multiple_of(owner * quarter, 16), quarter)
        for part in range(parts):
            lanes = slice(part * width, (part + 1) * width)
            w_gate[rows, lanes] = pack[part * quarter : (part + 1) * quarter, :]
            w_up[rows, lanes] = pack[(parts + part) * quarter : (parts + part + 1) * quarter, :]
        start = 2 * parts * quarter
        w_down[pl.ds(pl.multiple_of(owner * down_rows, 16), down_rows), :] = pack[
            start : start + down_rows, :
        ]
        w_out[rows, :] = pack[start + down_rows : start + down_rows + quarter, :]
    gain = vector_of(small, small_row + 1)
    readout = vector_of(small, small_row + 2)

    attended = attended_ref[...]
    residual = features_ref[...].astype(F32) + nn(attended, w_out[...])
    normed, inverse = rms(residual)
    hidden = (normed * gain).astype(BF16)
    gate = nn(hidden, w_gate[...])
    up = nn(hidden, w_up[...])
    sigmoid = jax.nn.sigmoid(gate)
    silu = gate * sigmoid
    activated = (silu * up).astype(BF16)
    outputs = residual + nn(activated, w_down[...])
    out_ref[...] = outputs
    energy = jnp.sum(outputs * readout, -1, keepdims=True)
    energy_ref[...] = jnp.broadcast_to(energy, (atoms, LANES)).T[:1, :]
    grad_energy = jnp.broadcast_to(grad_energy_ref[...], (LANES, atoms)).T[:, :1]
    grad_act = grad_out_ref[...].astype(F32) + grad_energy * readout
    grad_branch = grad_act.astype(BF16)
    g_down[...] = tn(activated, grad_branch)
    grad_activated = nt(grad_branch, w_down[...])
    grad_gate = (grad_activated * up * sigmoid * (1.0 + gate * (1.0 - sigmoid))).astype(BF16)
    grad_up = (grad_activated * silu).astype(BF16)
    g_gate[...] = tn(hidden, grad_gate)
    g_up[...] = tn(hidden, grad_up)
    grad_hidden = (nt(grad_gate, w_gate[...]) + nt(grad_up, w_up[...])).astype(BF16).astype(F32)
    grad_residual = grad_act + norm_back(grad_hidden * gain, normed, inverse)
    grad_residual_ref[...] = grad_residual
    grad_proj = grad_residual.astype(BF16)
    grad_attended_ref[...] = nt(grad_proj, w_out[...]).astype(BF16)
    g_out[...] = tn(attended, grad_proj)
    half = grads0.shape[0] // 2
    first = side_ref[0] * half
    for offset, grads in enumerate((grads0, grads1, grads2, grads3)):
        owner = lax.bitwise_xor(me, offset)
        rows = pl.ds(pl.multiple_of(owner * quarter, 16), quarter)
        pieces = []
        for grad in (g_gate, g_up):
            for part in range(parts):
                pieces.append(grad[rows, part * width : (part + 1) * width])
        down = pl.multiple_of(owner * down_rows, 16)
        pieces += [g_down[pl.ds(down, down_rows), :], g_out[rows, :]]
        row = 0
        for piece in pieces:
            for start in range(0, piece.shape[0], quarter // 2):
                other = row + half if row < half else row - half
                place = pl.multiple_of(jnp.where(first == 0, row, other), 16)
                grads[pl.ds(place, quarter // 2), :] = piece[start : start + quarter // 2].astype(
                    BF16
                )
                row += quarter // 2
    sums_ref[...] = jnp.zeros_like(sums_ref)
    sums_ref[1:2, :] = jnp.sum(grad_hidden * normed, 0, keepdims=True)
    sums_ref[2:3, :] = jnp.sum(grad_energy * outputs, 0, keepdims=True)


def ffn_call(index, side, features, attended, grad_out, grad_energy, small, packs, hidden, quarter, row):
    atoms, width = features.shape
    vmem = pl.BlockSpec(memory_space=pltpu.VMEM)
    return pl.pallas_call(
        functools.partial(ffn_kernel, quarter, row),
        out_shape=(
            jax.ShapeDtypeStruct((atoms, width), F32),
            jax.ShapeDtypeStruct((1, atoms), F32),
            jax.ShapeDtypeStruct((atoms, width), F32),
            jax.ShapeDtypeStruct((atoms, width), BF16),
            jax.ShapeDtypeStruct((8, width), F32),
        )
        + (jax.ShapeDtypeStruct(packs[0].shape, BF16),) * 4,
        in_specs=[pl.BlockSpec(memory_space=pltpu.SMEM)] * 2 + [vmem] * 12,
        out_specs=(vmem,) * 9,
        scratch_shapes=[
            pltpu.VMEM(shape, dtype)
            for dtype in (BF16, F32)
            for shape in ((width, hidden), (width, hidden), (hidden, width), (width, width))
        ],
        compiler_params=pltpu.CompilerParams(vmem_limit_bytes=24 * 2**20),
        cost_estimate=pl.CostEstimate(
            flops=18 * atoms * width * hidden, bytes_accessed=2**23, transcendentals=atoms * hidden
        ),
        name="feed_forward",
    )(index, side, features, attended, grad_out, grad_energy, *small, *packs)


def score_kernel(
    quarter,
    scale,
    index_ref,
    lookup_ref,
    query_ref,
    kvq_ref,
    pooled_ref,
    inverse_ref,
    attended_ref,
    grad_attended_ref,
    power_ref,
    edge_ref,
    grad_score_ref,
    mixed_ref,
    grad_query_ref,
    grads0,
    grads1,
    grads2,
    grads3,
    spread_q,
    spread_g,
    scaled,
    valued,
    means,
    bands,
    pooled,
    weight_grad,
):
    step = pl.program_id(0)
    atoms, width = query_ref.shape
    low_half = lax.broadcasted_iota(jnp.int32, (1, LANES), 1) < LANES // 2
    edges = edge_ref.shape[1]
    group_rows = bands.shape[1]
    groups = edges // GROUP
    pairs = GROUP // LANES

    @pl.when(step == 0)
    def _():
        grad_attended = grad_attended_ref[...].astype(F32)
        product = grad_attended * attended_ref[...].astype(F32)
        high = product.astype(BF16)
        low = (product - high.astype(F32)).astype(BF16)
        heads = lax.broadcasted_iota(jnp.int32, (width, HEADS * LANES), 0) // (width // HEADS)
        copies = lax.broadcasted_iota(jnp.int32, (width, HEADS * LANES), 1) // LANES
        summing = jnp.where(heads == copies, 1.0, 0.0).astype(BF16)
        mean = nn(high, summing) + nn(low, summing)
        for start in range(0, atoms, PAIRS):
            block, side = start // BLOCK, (start % BLOCK) // PAIRS
            for head in range(HEADS):
                place = block * BLOCK * HEADS + side * HEADS + head
                means[pl.ds(place, PAIRS, stride=2 * HEADS), :] = mean[
                    start : start + PAIRS, head * LANES : (head + 1) * LANES
                ]
        inverse = inverse_ref[...]
        means[...] = means[...] * inverse
        spread_heads(query_ref[...].astype(F32), pooled)
        spread_q[...] = wide(pooled).astype(BF16)
        spread_heads(grad_attended, pooled)
        spread_g[...] = wide(pooled).astype(BF16)
        scaled[...] = (wide(pooled) * jnp.concatenate([inverse] * (width // LANES), axis=1)).astype(
            BF16
        )
        valued[...] = nt(scaled[...], kvq_ref[2]).astype(BF16)
        bands[...] = jnp.zeros_like(bands)

    rows = BLOCK * HEADS
    base = pl.multiple_of(step * rows, rows)
    for group in range(groups):
        place = pl.ds(base + group * group_rows, group_rows)
        mixed_ref[group, :, :group_rows] = (nt(kvq_ref[1], spread_q[place, :]) * scale).astype(BF16)
        mixed_ref[group, :, group_rows:] = nt(kvq_ref[2], scaled[place, :]).astype(BF16)
    power = power_ref[...].astype(F32)
    for tile in range(edges // TILE):
        place = pl.ds(base + tile * 32, 32)
        product = nn(valued[place, :], edge_ref[:, tile * TILE : (tile + 1) * TILE])
        for side, grad_soft in enumerate(diagonal(product, low_half, means[place, :])):
            pair = 2 * tile + side
            own = slice(pair * 8, (pair + 1) * 8)
            group, column = pair // pairs, pair % pairs
            value = power[own] * grad_soft
            grad_score_ref[own, :] = value
            bands[
                group, column * 16 : (column + 1) * 16, column * LANES : (column + 1) * LANES
            ] = block_rows(value, low_half)
    for group in range(groups):
        result = nt(bands[group], edge_ref[:, group * GROUP : (group + 1) * GROUP])
        for half in range(width // LANES):
            pooled[half, pl.ds(base + group * group_rows, group_rows), :] = result[
                :, half * LANES : (half + 1) * LANES
            ]

    @pl.when(step == pl.num_programs(0) - 1)
    def _():
        grad_query = (gather_heads(pooled, kvq_ref[1], atoms) * scale).astype(BF16)
        grad_query_ref[...] = grad_query
        weight_grad[0] = tn(lookup_ref[HALO : HALO + atoms, :], grad_query)
        weight_grad[1] = tn(wide(pooled).astype(BF16), spread_q[...]) * scale
        weight_grad[2] = tn(pooled_ref[...], spread_g[...])
        me = index_ref[0]
        for offset, grads in enumerate((grads0, grads1, grads2, grads3)):
            owner = lax.bitwise_xor(me, offset)
            rows = pl.ds(pl.multiple_of(owner * quarter, 16), quarter)
            for which in range(3):
                grads[which * quarter : (which + 1) * quarter, :] = weight_grad[
                    which, rows, :
                ].astype(BF16)


def score_call(
    index, lookup, query, kvq, pooled, inverse, attended, grad_attended, power, edge, quarter
):
    atoms, width = query.shape
    blocks, _, edges = edge.shape
    head_rows = atoms * HEADS
    group_rows = GROUP // (edges // BLOCK) * HEADS
    groups = edges // GROUP
    full = lambda shape: pl.BlockSpec(shape, lambda b: (0,) * len(shape))
    whole = (lookup, query, kvq, pooled, inverse, attended, grad_attended)
    pair_block = pl.BlockSpec((None, PAIRS * HEADS, LANES), lambda b: (b, 0, 0))
    grads = (3 * quarter, width)
    return pl.pallas_call(
        functools.partial(score_kernel, quarter, (width // HEADS) ** -0.5),
        grid=(blocks,),
        out_shape=(
            jax.ShapeDtypeStruct((blocks, PAIRS * HEADS, LANES), F32),
            jax.ShapeDtypeStruct((blocks * groups, width, 2 * group_rows), BF16),
            jax.ShapeDtypeStruct((atoms, width), BF16),
        )
        + (jax.ShapeDtypeStruct(grads, BF16),) * 4,
        in_specs=[pl.BlockSpec(memory_space=pltpu.SMEM)]
        + [full(value.shape) for value in whole]
        + [pair_block, pl.BlockSpec((None, width, edges), lambda b: (b, 0, 0))],
        out_specs=(
            pair_block,
            pl.BlockSpec((groups, width, 2 * group_rows), lambda b: (b, 0, 0)),
            full((atoms, width)),
        )
        + (full(grads),) * 4,
        scratch_shapes=[
            pltpu.VMEM((head_rows, width), BF16),
            pltpu.VMEM((head_rows, width), BF16),
            pltpu.VMEM((head_rows, width), BF16),
            pltpu.VMEM((head_rows, width), BF16),
            pltpu.VMEM((head_rows, LANES), F32),
            pltpu.VMEM((groups, group_rows, GROUP), BF16),
            pltpu.VMEM((width // LANES, head_rows, LANES), F32),
            pltpu.VMEM((3, width, width), F32),
        ],
        compiler_params=pltpu.CompilerParams(vmem_limit_bytes=24 * 2**20),
        cost_estimate=pl.CostEstimate(
            flops=2 * atoms * edges // BLOCK * width * 256,
            bytes_accessed=2 * blocks * width * edges,
            transcendentals=0,
        ),
        name="score_backward",
    )(index, *whole, power, edge)


def edge_kernel(basis, gain_row, first_block, last_block, carried, final, *refs):
    refs = list(refs)
    take = lambda count: [refs.pop(0) for _ in range(count)]
    geometry, power_ref, grad_score_ref, mixed_ref = take(4)
    before = take(2 if carried else 0)
    if final:
        index_ref, features_ref, before_ref, after_ref, grad_query_ref, kvq_ref = take(6)
        grad_residual_ref, sums_ref = take(2)
        small = take(4)
        grad_own_ref, grad_lower_ref, grad_upper_ref = take(3)
        grads_refs = take(4)
    grad_rbf, grad_lookup = take(2)
    (bands,), grad_edges = take(1), take(len(refs) // 2)
    phis = refs
    block = pl.program_id(0) + first_block
    width = mixed_ref.shape[1]
    padded = basis[1]
    window = BLOCK + 2 * HALO
    low_half = lax.broadcasted_iota(jnp.int32, (1, LANES), 1) < LANES // 2
    group_rows = bands.shape[1] // 2
    groups = len(phis)
    pairs = GROUP // LANES

    @pl.when(block == first_block)
    def _():
        bands[...] = jnp.zeros_like(bands)
        if carried:
            grad_rbf[...] = before[0][...]
            grad_lookup[...] = before[1][...]
        else:
            grad_rbf[...] = jnp.zeros_like(grad_rbf)
            grad_lookup[...] = jnp.zeros_like(grad_lookup)

    power = power_ref[...].astype(F32)
    grad_score = grad_score_ref[...]
    for pair in range(PAIRS):
        group, column = pair // pairs, pair % pairs
        own = slice(pair * 8, (pair + 1) * 8)
        lanes = slice(column * LANES, (column + 1) * LANES)
        for start, value in ((0, grad_score[own]), (group_rows, power[own])):
            row = start + column * 16
            bands[group, row : row + 16, lanes] = block_rows(value, low_half)
    for group in range(groups):
        grad_edges[group][...] = nn(mixed_ref[group], bands[group]).astype(BF16)
    write_group(geometry, 0, basis, window, phis[0])
    total = None
    for group in range(groups):
        if group + 1 < groups:
            write_group(geometry, group + 1, basis, window, phis[group + 1])
        term = nt(phis[group][...], grad_edges[group][...])
        total = term if total is None else total + term
    grad_lookup[pl.ds(pl.multiple_of(block * BLOCK, BLOCK), window), :] += total[:window]
    grad_rbf[...] += total[window:]

    if not final:
        return

    @pl.when(block == last_block - 1)
    def _():
        atoms = features_ref.shape[0]
        grad_lookup[HALO : HALO + atoms, :] += nt(grad_query_ref[...], kvq_ref[0])
        gain = vector_of(small, gain_row)
        grad_gain = jnp.zeros((1, width), F32)
        places = (
            (before_ref, 0, grad_lower_ref),
            (features_ref, HALO, grad_own_ref),
            (after_ref, HALO + atoms, grad_upper_ref),
        )
        for ref, start, out in places:
            normed, inverse = rms(ref[...].astype(F32))
            grad = grad_lookup[start : start + ref.shape[0], :]
            grad_gain = grad_gain + jnp.sum(grad * normed, 0, keepdims=True)
            back = norm_back(grad * gain, normed, inverse)
            if start == HALO:
                back = back + grad_residual_ref[...]
            out[...] = back.astype(out.dtype)
        vectors = jnp.concatenate([grad_gain, sums_ref[1:8, :], jnp.zeros((8, width), F32)], 0)
        after_rbf = round_up(padded, 16)
        rest = jnp.zeros((after_rbf - padded, width), F32)
        me = index_ref[0]
        for offset, grads in enumerate(grads_refs):
            owner = lax.bitwise_xor(me, offset)
            rbf = grad_rbf[pl.ds(pl.multiple_of(owner * padded, 8), padded), :]
            grads[:after_rbf, :] = jnp.concatenate([rbf, rest], 0).astype(BF16)
            grads[after_rbf:, :] = vectors.astype(BF16)


def edge_call(arrays, carry, last, basis, members, gain_row, first_block, last_block):
    width = arrays[-1].shape[1]
    blocks = arrays[0].shape[0]
    rows, edges = members * basis[1], PAIRS * LANES
    groups = edges // GROUP
    group_rows = GROUP // (edges // BLOCK) * HEADS
    table = blocks * BLOCK + 2 * HALO
    window = BLOCK + 2 * HALO
    full = lambda shape: pl.BlockSpec(shape, lambda b: (0,) * len(shape))
    here = lambda b: (b + first_block, 0, 0)
    in_specs = [
        pl.BlockSpec((None, 3, PAIRS, LANES), lambda b: (b + first_block, 0, 0, 0)),
        pl.BlockSpec((None, PAIRS * HEADS, LANES), here),
        pl.BlockSpec((None, PAIRS * HEADS, LANES), here),
        pl.BlockSpec((groups, width, 2 * group_rows), here),
    ]
    operands = list(arrays)
    sums = [(rows, width), (table, width)]
    if carry is not None:
        in_specs += [full(value.shape) for value in carry]
        operands += list(carry)
    scratch = [pltpu.VMEM((groups, 2 * group_rows, GROUP), BF16)]
    scratch += [pltpu.VMEM((width, GROUP), BF16)] * groups
    scratch += [pltpu.VMEM((window + rows, GROUP), BF16)] * groups
    if last is None:
        shapes = [(shape, F32) for shape in sums]
    else:
        in_specs += [pl.BlockSpec(memory_space=pltpu.SMEM)]
        in_specs += [full(value.shape) for value in last[1:]]
        operands += list(last)
        grads = (round_up(basis[1], 16) + 16, width)
        shapes = [((blocks * BLOCK, width), F32)] + [((HALO, width), BF16)] * 2 + [(grads, BF16)] * 4
        scratch = [pltpu.VMEM(shape, F32) for shape in sums] + scratch
    return pl.pallas_call(
        functools.partial(
            edge_kernel, basis, gain_row, first_block, last_block, carry is not None, last is not None
        ),
        grid=(last_block - first_block,),
        out_shape=[jax.ShapeDtypeStruct(shape, dtype) for shape, dtype in shapes],
        in_specs=in_specs,
        out_specs=[full(shape) for shape, _ in shapes],
        scratch_shapes=scratch,
        compiler_params=pltpu.CompilerParams(vmem_limit_bytes=24 * 2**20),
        cost_estimate=pl.CostEstimate(
            flops=2 * (last_block - first_block) * edges * width * (rows + window + 256),
            bytes_accessed=2**22,
            transcendentals=(last_block - first_block) * rows * edges,
        ),
        name="edge_backward",
    )(*operands)


def early_kernel(
    side_ref,
    own_half,
    other_half,
    score_first,
    score_second,
    grad_own,
    from_lower,
    from_upper,
    gate,
    up,
    down,
    out,
    query,
    key,
    value,
    features,
    total,
):
    half = own_half.shape[0]
    own = side_ref[0]
    total[pl.ds(pl.multiple_of(own * half, 16), half), :] = own_half[...].astype(F32)
    total[pl.ds(pl.multiple_of((1 - own) * half, 16), half), :] = other_half[...].astype(F32)
    quarter, width = out.shape
    row = 0
    for ref in (gate, up):
        for part in range(ref.shape[1] // width):
            ref[:, part * width : (part + 1) * width] = total[row : row + quarter, :]
            row += quarter
    for ref in (down, out):
        ref[...] = total[row : row + ref.shape[0], :]
        row += ref.shape[0]
    for which, ref in enumerate((query, key, value)):
        rows = slice(which * quarter, (which + 1) * quarter)
        ref[...] = score_first[rows, :].astype(F32) + score_second[rows, :].astype(F32)
    features[...] = grad_own[...]
    features[:HALO, :] += from_lower[...].astype(F32)
    features[features.shape[0] - HALO :, :] += from_upper[...].astype(F32)


def early_call(side, halves, score, grad_own, from_lower, from_upper, quarter, hidden, down_rows):
    rows, width = halves[0].shape
    vmem = pl.BlockSpec(memory_space=pltpu.VMEM)
    shapes = [(quarter, hidden)] * 2 + [(down_rows, width)] + [(quarter, width)] * 4
    shapes += [grad_own.shape]
    return pl.pallas_call(
        early_kernel,
        out_shape=[jax.ShapeDtypeStruct(shape, F32) for shape in shapes],
        in_specs=[pl.BlockSpec(memory_space=pltpu.SMEM)] + [vmem] * 7,
        out_specs=[vmem] * 8,
        scratch_shapes=[pltpu.VMEM((2 * rows, width), F32)],
        name="early_results",
    )(side, *halves, *score, grad_own, from_lower, from_upper)


def last_kernel(index_ref, first, second, rbf, gain_attn, gain_ffn, readout):
    total = first[...].astype(F32) + second[...].astype(F32)
    rbf[...] = total[: rbf.shape[0]]
    start, width = first.shape[0] - 16, first.shape[1]
    quarter = readout.shape[1]
    me = index_ref[0]
    for which, ref in enumerate((gain_attn, gain_ffn, readout)):
        row = total[start + which : start + which + 1]
        picked = jnp.zeros((1, quarter), F32)
        for owner in range(width // quarter):
            piece = row[:, owner * quarter : (owner + 1) * quarter]
            picked = picked + jnp.where(me == owner, piece, 0.0)
        ref[...] = picked


def last_call(index, terms, shard, quarter):
    width = terms[0].shape[1]
    vmem = pl.BlockSpec(memory_space=pltpu.VMEM)
    shapes = [(shard, width)] + [(1, quarter)] * 3
    return pl.pallas_call(
        last_kernel,
        out_shape=[jax.ShapeDtypeStruct(shape, F32) for shape in shapes],
        in_specs=[pl.BlockSpec(memory_space=pltpu.SMEM)] + [vmem] * 2,
        out_specs=[vmem] * 4,
        name="last_results",
    )(index, *terms)


def exchange(value, axis, offset):
    size = lax.axis_size(axis)
    return lax.ppermute(value, axis, [(i, i ^ offset) for i in range(size)])


def shifted(value, by):
    axes = ("space", "wt")
    size = lax.axis_size(axes)
    pairs = [(i, i + by) for i in range(size) if 0 <= i + by < size]
    return lax.ppermute(value, axes, pairs)


def gathered(value):
    return [value] + [exchange(value, "wt", offset) for offset in range(1, lax.axis_size("wt"))]


def added(*values):
    total = values[0].astype(F32)
    for value in values[1:]:
        total = total + value.astype(F32)
    return total.astype(values[0].dtype)


class Reduction:
    def __init__(self, chunks, halved=False):
        self.halved = halved
        self.sent = 0
        self.steps = lax.axis_size("space").bit_length() - 1
        self.terms = [chunks[0]] + [
            exchange(chunk, "wt", offset) for offset, chunk in enumerate(chunks[1:], 1)
        ]

    def done(self):
        return self.sent == self.steps + (1 if self.halved else 0)

    def add(self):
        if not self.done():
            self.terms = [added(*self.terms)]

    def send(self):
        if self.done():
            return
        (value,) = self.terms
        if self.sent == self.steps:
            self.terms.append(exchange(value, "space", 1))
        elif self.sent == 0 and self.halved:
            rows = value.shape[0] // 2
            self.terms = [value[:rows], exchange(value[rows:], "space", 1)]
        else:
            self.terms.append(exchange(value, "space", 1 << self.sent))
        self.sent += 1

    def finish(self):
        while not self.done():
            self.add()
            self.send()
        return self.terms


def between(reductions, value):
    terms = [reduction.terms for reduction in reductions]
    terms, value = lax.optimization_barrier((terms, value))
    for reduction, own in zip(reductions, terms):
        reduction.terms = list(own)
        reduction.add()
    terms = [reduction.terms for reduction in reductions]
    terms, value = lax.optimization_barrier((terms, value))
    for reduction, own in zip(reductions, terms):
        reduction.terms = list(own)
        reduction.send()
    return value


SPLIT = (2, 2, 2)


def local(
    features,
    distances,
    neighbours,
    counts,
    rbf_weight,
    query_weight,
    key_weight,
    value_weight,
    out_weight,
    gate_weight,
    up_weight,
    down_weight,
    attn_gain,
    ffn_gain,
    readout,
    grad_out,
    grad_energy,
):
    members = lax.axis_size("wt")
    atoms, width = features.shape
    shard = rbf_weight.shape[0]
    padded = round_up(shard, 8)
    factor = basis_factor(members * shard)
    basis = (shard, padded, factor * CUTOFF / (members * shard))
    gain_row = round_up(shard, 16) + 3 * query_weight.shape[0]
    quarter = query_weight.shape[0]
    hidden = gate_weight.shape[1]
    index = lax.axis_index("wt").astype(jnp.int32)[None]
    side = (lax.axis_index("space") % 2).astype(jnp.int32)[None]

    small, large, initial, final = pack_call(
        index,
        rbf_weight,
        query_weight,
        key_weight,
        value_weight,
        out_weight,
        gate_weight,
        up_weight,
        down_weight,
        attn_gain[None],
        ffn_gain[None],
        readout[None],
        features,
    )
    small_all = gathered(small)
    before = shifted(final, 1)
    after = shifted(initial, -1)
    geometry, done = geometry_call(distances.T, neighbours.T, factor)
    large, _ = lax.optimization_barrier((large, done))
    large_all = gathered(large)

    edge, power, inverse, pooled, attended, lookup, query, kvq = forward_call(
        index, counts, features, before, after, small_all, geometry, basis, quarter
    )
    outputs, energy, grad_residual, grad_attended, sums, *large_grads = ffn_call(
        index,
        side,
        features,
        attended,
        grad_out,
        grad_energy[None, :],
        small_all,
        large_all,
        hidden,
        quarter,
        gain_row,
    )
    grad_score, mixed, grad_query, *score_grads = score_call(
        index, lookup, query, kvq, pooled, inverse, attended, grad_attended, power, edge, quarter
    )
    large_sum, score_sum = Reduction(large_grads, True), Reduction(score_grads)
    carry, block = None, 0
    last = (index, features, before, after, grad_query, kvq, grad_residual, sums, *small_all)
    for count in SPLIT:
        if carry is None:
            grad_score = between([large_sum], grad_score)
        else:
            carry = between([large_sum, score_sum], carry)
        final = block + count == edge.shape[0]
        carry = edge_call(
            (geometry, power, grad_score, mixed),
            carry,
            last if final else None,
            basis,
            members,
            gain_row,
            block,
            block + count,
        )
        block += count
    grad_own, grad_lower, grad_upper, *edge_grads = carry
    edge_sum = Reduction(edge_grads)
    from_upper = shifted(grad_lower, -1)
    from_lower = shifted(grad_upper, 1)
    between([edge_sum, large_sum], ())
    large_sum, score_sum, from_upper, from_lower = between(
        [edge_sum], (large_sum.finish(), score_sum.finish(), from_upper, from_lower)
    )
    results = early_call(
        side,
        large_sum,
        score_sum,
        grad_own,
        from_lower,
        from_upper,
        quarter,
        hidden,
        down_weight.shape[0],
    )
    grad_gate, grad_up, grad_down, grad_out_w, grad_q, grad_k, grad_v, grad_features = between(
        [edge_sum], results
    )
    grad_rbf, grad_attn, grad_ffn, grad_read = last_call(
        index, edge_sum.finish(), shard, quarter
    )
    return (
        outputs,
        energy[0],
        grad_features,
        grad_rbf,
        grad_q,
        grad_k,
        grad_v,
        grad_out_w,
        grad_gate,
        grad_up,
        grad_down,
        grad_attn[0],
        grad_ffn[0],
        grad_read[0],
    )


def solution(mesh):
    rows = P(("space", "wt"), None)
    line = P(("space", "wt"))
    in_specs = (rows, rows, rows, line) + (P("wt", None),) * 8 + (P("wt"),) * 3 + (rows, line)
    out_specs = (rows, line, rows) + (P("wt", None),) * 8 + (P("wt"),) * 3
    return jax.shard_map(local, mesh=mesh, in_specs=in_specs, out_specs=out_specs, check_vma=False)
```
